1024 devices in a mesh: group: 64 (over x, z), shard: 16 (over y, core).
Axes of the slice: x: 4, y: 8, z: 16, core: 2. Of those that a mesh axis runs over, the one named last changes fastest.
Arguments:
- embeddings: bfloat16 [524288, 768], P(('group', 'shard')), may hold values from -1000 to 1000
- cluster_id: int32 [524288], P(('group', 'shard')), may hold values from 0 to 127, as said below
- row_index: int32 [524288], P(('group', 'shard')), may hold values from 0 to 524287, each once
Outputs:
- best: float32 [524288], P(('group', 'shard'))
The draws below stay inside these ranges and needn't reach their ends.
Inputs may be any that keep to these rules, and one draw needn't show every extreme that they name: `cluster_id`: cluster c of a group is owned by shard index c // 8. The rows of one device name clusters of one owner at most 64 times, and in every group one owner is named exactly 64 times by the rows of each device of the group.
All inputs are finite; a program needn't handle non-finite values.
Results may differ from the reference program's by a relative error of at most 0.00059.
Values may be sent and summed in bfloat16 or wider, within the bound.
No kernel may reach another device: no remote copies, remote signals or barrier semaphores. Data moves between devices by JAX's collectives and lax.ppermute only.
A program may use at most 64 MiB of HBM per device.

```python
import math
import jax
import jax.numpy as jnp
from jax import lax

D = 768
R_DEV = 512
CL_OWN = 8
CAP = 64
SLOTS = 1024
GROUP_ROWS = 8192
ROWS = 524288
CLUSTERS = 128
N_GROUP = 64
N_SHARD = 16


def cluster_draw(key):
    blocks = ROWS // R_DEV
    groups = blocks // N_SHARD
    keys = jax.random.split(key, 4)
    tickets_all = N_SHARD * CAP
    hottest = jax.random.randint(keys[0], (groups,), 0, N_SHARD)
    hot_block = jnp.repeat(hottest, N_SHARD)
    tickets = jnp.arange(tickets_all, dtype=jnp.int32) // CAP
    scores = jax.random.randint(keys[1], (blocks, tickets_all), 0, 2 ** 20) * tickets_all + jnp.arange(tickets_all, dtype=jnp.int32)[None, :]
    scores = jnp.where(tickets[None, :] == hot_block[:, None], scores - 2 ** 30, scores)
    picked = jnp.argsort(scores, axis=1)[:, :R_DEV]
    owners = tickets[picked]
    owners = jax.vmap(jax.random.permutation)(jax.random.split(keys[2], blocks), owners)
    within = jax.random.randint(keys[3], (blocks, R_DEV), 0, CL_OWN)
    return (owners * CL_OWN + within).reshape(ROWS).astype(jnp.int32)


def draw_cluster_id(key, part):
    return cluster_draw(key)


def draw_embeddings(key, part):
    clusters = cluster_draw(key)
    key = jax.random.fold_in(key, 7)
    keys = jax.random.split(key, 5)
    blocks = ROWS // R_DEV
    column_scale = jnp.exp(jax.random.uniform(keys[0], (D,), jnp.float32, 0.0, math.log(10.0)))
    noise = jnp.clip(jax.random.normal(keys[1], (ROWS, D), jnp.float32), -4.0, 4.0)
    centroids = jnp.clip(jax.random.normal(keys[2], (CLUSTERS, D), jnp.float32), -4.0, 4.0)
    tilt_power = jax.random.uniform(keys[3], (D,), jnp.float32, -1.0, 1.0)
    offset = 0.5 * jnp.clip(jax.random.normal(keys[4], (D,), jnp.float32), -4.0, 4.0)
    fraction = (jnp.arange(ROWS) // R_DEV).astype(jnp.float32) / max(blocks - 1, 1)
    growth = 1.0 + 2.0 * fraction
    tilted = growth[:, None] ** tilt_power[None, :]
    base = 0.8 * centroids[clusters] + 0.6 * noise + offset[None, :]
    values = column_scale[None, :] * tilted * jnp.sqrt(growth)[:, None] * base
    return jnp.clip(values, -1000.0, 1000.0).astype(jnp.bfloat16)


def setup_inputs(seed: int = 0) -> dict:
    seeds = jax.random.split(jax.random.key(seed), 4)
    embeddings = draw_embeddings(jax.random.fold_in(seeds[3], 71), 0)
    cluster_id = draw_cluster_id(jax.random.fold_in(seeds[3], 71), 0)
    row_index = jax.random.permutation(seeds[2], ROWS).astype(jnp.int32)
    return {"embeddings": embeddings, "cluster_id": cluster_id, "row_index": row_index}


def unit_rows(raw, column_mean, factor_low):
    centered = raw.astype(jnp.float32) - column_mean[None, :]
    whitened = jax.scipy.linalg.solve_triangular(factor_low, centered.T, lower=True).T
    scaling = lax.rsqrt(lax.optimization_barrier(jnp.sum(whitened * whitened, axis=1, keepdims=True)) + 1e-06)
    return (whitened * scaling).astype(jnp.bfloat16)

def masked_max(queries, query_cluster, query_index, keyset, key_cluster, key_index):
    scores = lax.dot_general(queries.astype(jnp.float32), keyset.astype(jnp.float32), (((1,), (1,)), ((), ())), preferred_element_type=jnp.float32)
    allowed = (query_cluster[:, None] == key_cluster[None, :]) & (query_cluster[:, None] >= 0)
    allowed = allowed & (key_index[None, :] < query_index[:, None])
    return lax.optimization_barrier(jnp.max(jnp.where(allowed, scores, -1.0), axis=1))

def group_best(packed):
    units, clusters, indices = packed
    sorted_order = jnp.argsort(clusters, stable=True).astype(jnp.int32)
    sorted_units = jnp.concatenate([units[sorted_order], jnp.zeros((SLOTS, D), units.dtype)], axis=0)
    sorted_clusters = jnp.concatenate([clusters[sorted_order], jnp.full((SLOTS,), -1, jnp.int32)])
    sorted_index = jnp.concatenate([indices[sorted_order], jnp.zeros((SLOTS,), jnp.int32)])
    owner_of = (clusters[sorted_order] // CL_OWN).astype(jnp.int32)
    member = (owner_of[:, None] == jnp.arange(N_SHARD, dtype=jnp.int32)[None, :]).astype(jnp.int32)
    counts = lax.optimization_barrier(jnp.sum(member, axis=0))
    offsets = (jnp.cumsum(counts) - counts).astype(jnp.int32)

    def owner_best(offset):
        block_units = lax.dynamic_slice_in_dim(sorted_units, offset, SLOTS, 0)
        block_cluster = lax.dynamic_slice_in_dim(sorted_clusters, offset, SLOTS, 0)
        block_index = lax.dynamic_slice_in_dim(sorted_index, offset, SLOTS, 0)
        return masked_max(block_units, block_cluster, block_index, block_units, block_cluster, block_index)
    results = lax.map(owner_best, offsets)
    position = jnp.arange(GROUP_ROWS, dtype=jnp.int32) - offsets[owner_of]
    sorted_best = results[owner_of, position]
    return jnp.zeros((GROUP_ROWS,), jnp.float32).at[sorted_order].set(sorted_best.astype(jnp.float32))

def reference(embeddings, cluster_id, row_index):
    column_sums = lax.optimization_barrier(jnp.sum(embeddings, axis=0, dtype=jnp.float32))
    second = jnp.dot(embeddings.T.astype(jnp.float32), embeddings.astype(jnp.float32), preferred_element_type=jnp.float32)
    column_mean = column_sums / ROWS
    covariance = second / ROWS - column_mean[:, None] * column_mean[None, :]
    factor_low = jnp.linalg.cholesky(covariance)
    units = unit_rows(embeddings, column_mean, factor_low)
    best = lax.map(group_best, (units.reshape(N_GROUP, GROUP_ROWS, D), cluster_id.reshape(N_GROUP, GROUP_ROWS), row_index.reshape(N_GROUP, GROUP_ROWS)))
    return best.reshape(ROWS)
```

```python
import functools

import jax
import jax.numpy as jnp
from jax import lax
from jax.experimental import pallas as pl
from jax.experimental.pallas import tpu as pltpu
from jax.sharding import Mesh, PartitionSpec as P

F32 = jnp.float32
BF16 = jnp.bfloat16
FEAT = 768
BLK = 128
NBLK = FEAT // BLK
PANELS = BLK // 8
PAIRS = [(i, j) for i in range(NBLK) for j in range(i + 1)]
HALF = 12 * BLK
CAP = 64
CL_OWN = 8
INDEX_SPAN = 2**19
EMPTY = 2**30
HIGHEST = lax.Precision.HIGHEST
VM = pl.BlockSpec(memory_space=pltpu.VMEM)
SM = pl.BlockSpec(memory_space=pltpu.SMEM)
PARAMS = pltpu.CompilerParams(vmem_limit_bytes=48 * 2**20)


def nt(a, b, precision=None):
    return lax.dot_general(
        a, b, (((1,), (1,)), ((), ())), precision=precision, preferred_element_type=F32
    )


def nn(a, b, precision=None):
    return lax.dot_general(
        a, b, (((1,), (0,)), ((), ())), precision=precision, preferred_element_type=F32
    )


def split3(x):
    high = x.astype(BF16)
    rest = x - high.astype(F32)
    mid = rest.astype(BF16)
    low = (rest - mid.astype(F32)).astype(BF16)
    return high, mid, low


def moments_kernel(core_ref, x_ref, keep_ref, send_ref, tri_ref, sems):
    x = x_ref[...]
    sums = nn(jnp.ones((8, x.shape[0]), BF16), x)
    for i2 in range(NBLK // 2):
        left = x[:, 256 * i2 : 256 * (i2 + 1)].T
        wide = nn(left, x[:, : 256 * (i2 + 1)])
        for i in (2 * i2, 2 * i2 + 1):
            for j in range(i + 1):
                spot = PAIRS.index((i, j))
                row = BLK * (i - 2 * i2)
                tri_ref[spot // 12, BLK * (spot % 12) : BLK * (spot % 12 + 1), :] = wide[
                    row : row + BLK, BLK * j : BLK * (j + 1)
                ]
    base = BLK * (len(PAIRS) - 12)
    tri_ref[1, base:HALF, :] = jnp.zeros((HALF - base, BLK), F32)
    for j in range(NBLK):
        tri_ref[1, base + 8 * j : base + 8 * j + 8, :] = sums[:, BLK * j : BLK * (j + 1)]
    core = core_ref[0]
    mine = pltpu.make_async_copy(tri_ref.at[core], keep_ref, sems.at[0])
    other = pltpu.make_async_copy(tri_ref.at[1 - core], send_ref, sems.at[1])
    other.start()
    mine.start()
    other.wait()
    mine.wait()


def moments(core, x):
    half = jax.ShapeDtypeStruct((HALF, BLK), F32)
    return pl.pallas_call(
        moments_kernel,
        out_shape=(half, half),
        in_specs=[SM, VM],
        out_specs=(pl.BlockSpec(memory_space=pl.ANY), pl.BlockSpec(memory_space=pl.ANY)),
        scratch_shapes=[pltpu.VMEM((2, HALF, BLK), F32), pltpu.SemaphoreType.DMA((2,))],
        compiler_params=PARAMS,
        name="moments",
    )(core, x)


def pack_kernel(x_ref, cluster_ref, index_ref, rows_ref, key_ref, slot_ref):
    count = x_ref.shape[0]
    slots = rows_ref.shape[0]
    owners = slots // CAP
    cluster = cluster_ref[...]
    owner = cluster // CL_OWN
    member = lax.broadcasted_iota(jnp.int32, (owners, count), 0) == jnp.broadcast_to(
        owner, (owners, count)
    )
    earlier = (
        lax.broadcasted_iota(jnp.int32, (count, count), 0)
        < lax.broadcasted_iota(jnp.int32, (count, count), 1)
    )
    prefix = nn(jnp.where(member, 1.0, 0.0).astype(BF16), jnp.where(earlier, 1.0, 0.0).astype(BF16))
    rank = jnp.sum(jnp.where(member, prefix, 0.0), axis=0, keepdims=True).astype(jnp.int32)
    slot = owner * CAP + rank
    slot_ref[...] = slot
    place = jnp.where(
        lax.broadcasted_iota(jnp.int32, (slots, count), 0) == jnp.broadcast_to(slot, (slots, count)),
        1.0,
        0.0,
    ).astype(BF16)
    rows_ref[...] = nn(place, x_ref[...]).astype(BF16)
    key = cluster * INDEX_SPAN + index_ref[...]
    digit = lax.broadcasted_iota(jnp.int32, (8, count), 0)
    whole = jnp.broadcast_to(key, (8, count))
    parts = jnp.where(digit < 4, (whole >> (7 * jnp.minimum(digit, 3))) & 127, 1)
    moved = nt(parts.astype(F32).astype(BF16), place)
    back = moved.astype(jnp.int32)
    full = back[0:1] + (back[1:2] << 7) + (back[2:3] << 14) + (back[3:4] << 21)
    key_ref[...] = jnp.where(back[4:5] > 0, full, EMPTY)


def pack(x, cluster_id, row_index, owners):
    count = x.shape[0]
    slots = owners * CAP
    return pl.pallas_call(
        pack_kernel,
        out_shape=(
            jax.ShapeDtypeStruct((slots, FEAT), BF16),
            jax.ShapeDtypeStruct((1, slots), jnp.int32),
            jax.ShapeDtypeStruct((1, count), jnp.int32),
        ),
        in_specs=[VM, VM, VM],
        out_specs=(VM, VM, VM),
        compiler_params=PARAMS,
        name="pack_rows",
    )(x, cluster_id.reshape(1, count), row_index.reshape(1, count))


def reciprocal(x):
    r = pl.reciprocal(x, approx=True)
    r = r * (2.0 - x * r)
    return r * (2.0 - x * r)


def inverse_factor(a):
    lane = lax.broadcasted_iota(jnp.int32, (8, BLK), 1)
    sub = lax.broadcasted_iota(jnp.int32, (8, BLK), 0)
    w = [jnp.where(lane == sub + 8 * g, 1.0, 0.0).astype(F32) for g in range(PANELS)]
    out = []

    def row(x, k):
        return jnp.broadcast_to(x[k : k + 1, :], (8, BLK))

    def column(x, k):
        return jnp.broadcast_to(x[:, k : k + 1], (8, BLK))

    for g in range(PANELS):
        d = [column(a[g], 8 * g + k) for k in range(8)]
        m = {h: [column(a[h], 8 * g + k) for k in range(8)] for h in range(g + 1, PANELS)}
        s = {(k, l): row(d[l], k) for k in range(8) for l in range(k, 8)}
        scale = [None] * 8
        for k in range(0, 8, 2):
            p, q, t = s[k, k], s[k, k + 1], s[k + 1, k + 1]
            det = p * t - q * q
            over = reciprocal(det)
            ip, iq, it = t * over, q * over, p * over
            over_p = reciprocal(p)
            scale[k] = lax.rsqrt(p)
            scale[k + 1] = lax.rsqrt(det * over_p)
            for l in range(k + 2, 8):
                al = s[k, l] * ip - s[k + 1, l] * iq
                be = s[k + 1, l] * it - s[k, l] * iq
                for n in range(l, 8):
                    s[l, n] = s[l, n] - (al * s[k, n] + be * s[k + 1, n])
            a0, a1, w0, w1 = row(a[g], k), row(a[g], k + 1), row(w[g], k), row(w[g], k + 1)
            ma = jnp.where(sub > k + 1, d[k] * ip - d[k + 1] * iq, 0.0)
            mb = jnp.where(sub > k + 1, d[k + 1] * it - d[k] * iq, 0.0)
            for l in range(k + 2, 8):
                d[l] = d[l] - (ma * s[k, l] + mb * s[k + 1, l])
            if k < 6:
                a[g] = a[g] - (ma * a0 + mb * a1)
            mw = jnp.where(sub == k + 1, q * over_p, ma)
            w[g] = w[g] - (mw * w0 + mb * w1)
            for h in range(g + 1, PANELS):
                ha = m[h][k] * ip - m[h][k + 1] * iq
                hb = m[h][k + 1] * it - m[h][k] * iq
                for l in range(k + 2, 8):
                    m[h][l] = m[h][l] - (ha * s[k, l] + hb * s[k + 1, l])
                a[h] = a[h] - (ha * a0 + hb * a1)
                w[h] = w[h] - (ha * w0 + hb * w1)
        scales = scale[0]
        for k in range(1, 8):
            scales = jnp.where(sub == k, scale[k], scales)
        out.append(w[g] * scales)
    return jnp.concatenate(out, axis=0)


def factor_kernel(total_rows, core_ref, mine_ref, other_ref, high_ref, mid_ref, low_ref, mean_ref, s_ref, w_ref):
    core = core_ref[0]
    first_sums = BLK * (len(PAIRS) - 12)

    def assemble(halves):
        sums = halves[1][first_sums : first_sums + BLK, :] * (1.0 / total_rows)
        means = [sums[8 * j : 8 * j + 1, :] for j in range(NBLK)]
        turned = sums.T
        for spot, (i, j) in enumerate(PAIRS):
            at = BLK * (spot % 12)
            block = halves[spot // 12][at : at + BLK, :] * (1.0 / total_rows)
            s_ref[BLK * i : BLK * (i + 1), BLK * j : BLK * (j + 1)] = (
                block - turned[:, 8 * i : 8 * i + 1] * means[j]
            )
        parts = split3(jnp.concatenate(means, axis=1))
        mean_ref[...] = jnp.concatenate(
            [p.astype(F32) for p in parts] + [jnp.zeros((13, FEAT), F32)], axis=0
        ).astype(BF16)

    @pl.when(core == 0)
    def _():
        assemble((mine_ref, other_ref))

    @pl.when(core == 1)
    def _():
        assemble((other_ref, mine_ref))

    w_ref[...] = jnp.zeros((FEAT, FEAT), F32)
    for k in range(NBLK):
        at, to = BLK * k, BLK * (k + 1)
        inv = inverse_factor([s_ref[at + 8 * g : at + 8 * g + 8, at:to] for g in range(PANELS)])
        if k:
            w_ref[at:to, :at] = nn(inv, w_ref[at:to, :at], HIGHEST)
        w_ref[at:to, at:to] = inv
        if to < FEAT:
            below = nt(s_ref[to:, at:to], inv, HIGHEST)
            s_ref[to:, to:] = s_ref[to:, to:] - nt(below, below, HIGHEST)
            w_ref[to:, :to] = w_ref[to:, :to] - nn(below, w_ref[at:to, :to], HIGHEST)
    high_ref[...], mid_ref[...], low_ref[...] = split3(w_ref[...])


def factor(core, mine, other, total_rows):
    square = jax.ShapeDtypeStruct((FEAT, FEAT), BF16)
    return pl.pallas_call(
        functools.partial(factor_kernel, total_rows),
        out_shape=(square, square, square, jax.ShapeDtypeStruct((16, FEAT), BF16)),
        in_specs=[SM, VM, VM],
        out_specs=(VM, VM, VM, VM),
        scratch_shapes=[pltpu.VMEM((FEAT, FEAT), F32), pltpu.VMEM((FEAT, FEAT), F32)],
        compiler_params=PARAMS,
        name="factor",
    )(core, mine, other)


def best_kernel(x_ref, high_ref, mid_ref, low_ref, mean_ref, qkey_ref, kkey_ref, best_ref, z_ref, u_ref):
    slots = x_ref.shape[0]
    x = jnp.concatenate([x_ref[...], mean_ref[...]], axis=0)
    norm = jnp.zeros((slots, 1), F32)
    for n in range(FEAT // 256):
        at, to = 256 * n, 256 * (n + 1)
        z = (
            nt(x[:, :to], low_ref[at:to, :to])
            + nt(x[:, :to], mid_ref[at:to, :to])
            + nt(x[:, :to], high_ref[at:to, :to])
        )
        z = z[:slots] - jnp.sum(z[slots:], axis=0, keepdims=True)
        norm = norm + jnp.sum(z * z, axis=1, keepdims=True)
        z_ref[:, at:to] = z
    u_ref[...] = (z_ref[...] * lax.rsqrt(norm + 1e-06)).astype(BF16)
    qkey = qkey_ref[...]
    floor = qkey & ~(INDEX_SPAN - 1)
    best = jnp.full((1, slots), -1.0, F32)
    rows = 256
    for b in range(slots // rows):
        scores = nt(u_ref[rows * b : rows * (b + 1), :], u_ref[...])
        kkey = kkey_ref[rows * b : rows * (b + 1), :]
        allowed = (kkey < qkey) & (kkey >= floor)
        best = jnp.maximum(best, jnp.max(jnp.where(allowed, scores, -1.0), axis=0, keepdims=True))
    best_ref[...] = best


def best_of(x, high, mid, low, mean, keys):
    slots = x.shape[0]
    return pl.pallas_call(
        best_kernel,
        out_shape=jax.ShapeDtypeStruct((1, slots), F32),
        in_specs=[VM] * 7,
        out_specs=VM,
        scratch_shapes=[pltpu.VMEM((slots, FEAT), F32), pltpu.VMEM((slots, FEAT), BF16)],
        compiler_params=PARAMS,
        name="best",
    )(x, high, mid, low, mean, keys.reshape(1, slots), keys.reshape(slots, 1))


def unpack_kernel(best_ref, slot_ref, out_ref):
    best = best_ref[...]
    owners = best.shape[0]
    count = slot_ref.shape[1]
    slot = slot_ref[...]
    rank = jnp.broadcast_to(slot % CAP, (CAP, count))
    pick = jnp.where(lax.broadcasted_iota(jnp.int32, (CAP, count), 0) == rank, 1.0, 0.0)
    table = nn(best, pick.astype(F32), HIGHEST)
    owner = jnp.broadcast_to(slot // CAP, (owners, count))
    mine = lax.broadcasted_iota(jnp.int32, (owners, count), 0) == owner
    out_ref[...] = jnp.sum(jnp.where(mine, table, 0.0), axis=0, keepdims=True)


def unpack(best, slot):
    return pl.pallas_call(
        unpack_kernel,
        out_shape=jax.ShapeDtypeStruct(slot.shape, F32),
        in_specs=[VM, VM],
        out_specs=VM,
        compiler_params=PARAMS,
        name="unpack",
    )(best, slot)


def exchange(x, axis):
    return lax.all_to_all(x, axis, split_axis=0, concat_axis=0, tiled=True)


def on_device(embeddings, cluster_id, row_index):
    count = embeddings.shape[0]
    groups, highs = lax.axis_size("group"), lax.axis_size("y")
    owners = 2 * highs
    total_rows = count * owners * groups
    shard = ("y", "core")
    swap = [(0, 1), (1, 0)]
    core = lax.axis_index("core").astype(jnp.int32).reshape(1)
    keep, send = moments(core, embeddings)
    pair = keep + lax.ppermute(send, "core", swap)
    share = HALF // groups
    spread = exchange(pair.reshape(groups, share, BLK), "group")
    packed, key, slot = pack(embeddings, cluster_id, row_index, owners)
    part = jnp.sum(spread, axis=0)
    rows_y = exchange(jnp.broadcast_to(part[None], (highs, share, BLK)), "y")
    total = jnp.sum(rows_y, axis=0)
    mine = exchange(jnp.broadcast_to(total[None], (groups, share, BLK)), "group").reshape(HALF, BLK)
    packed, key, total = lax.optimization_barrier((packed, key, total))
    arrived = exchange(packed.reshape(owners, CAP, FEAT), shard).reshape(owners * CAP, FEAT)
    keys = exchange(key.reshape(owners, CAP), shard).reshape(owners * CAP)
    other = lax.ppermute(mine, "core", swap)
    high, mid, low, mean = factor(core, mine, other, total_rows)
    best = best_of(arrived, high, mid, low, mean, keys)
    returned = exchange(best.reshape(owners, CAP), shard)
    return unpack(returned, slot).reshape(count)


def solution(mesh):
    groups, shards = mesh.devices.shape
    split = Mesh(mesh.devices.reshape(groups, shards // 2, 2), ("group", "y", "core"))
    rows = ("group", "y", "core")
    return jax.shard_map(
        on_device,
        mesh=split,
        in_specs=(P(rows, None), P(rows), P(rows)),
        out_specs=P(rows),
        check_vma=False,
    )
```

```python
import functools

import jax
import jax.numpy as jnp
from jax import lax
from jax.experimental import pallas as pl
from jax.experimental.pallas import tpu as pltpu
from jax.sharding import Mesh, PartitionSpec as P

F32 = jnp.float32
BF16 = jnp.bfloat16
FEAT = 768
BLK = 64
NBLK = FEAT // BLK
PANELS = BLK // 8
LANES = 128
WHOLE = [(i, j) for i in range(NBLK) for j in range((i + 1) // 2)]
PAIRED = [(i, i + 2) for i in range(0, NBLK, 4)]
TILES = len(WHOLE) + len(PAIRED) + 1
HALF = TILES // 2 * BLK
WIDE = FEAT + LANES
CAP = 64
CL_OWN = 8
INDEX_SPAN = 2**19
PIECES = 2
HIGHEST = lax.Precision.HIGHEST
VM = pl.BlockSpec(memory_space=pltpu.VMEM)
SM = pl.BlockSpec(memory_space=pltpu.SMEM)
ANY = pl.BlockSpec(memory_space=pl.ANY)
PARAMS = pltpu.CompilerParams(vmem_limit_bytes=24 * 2**20)


def nt(a, b, precision=None):
    return lax.dot_general(
        a, b, (((1,), (1,)), ((), ())), precision=precision, preferred_element_type=F32
    )


def nn(a, b, precision=None):
    return lax.dot_general(
        a, b, (((1,), (0,)), ((), ())), precision=precision, preferred_element_type=F32
    )


def split3(x):
    high = x.astype(BF16)
    rest = x - high.astype(F32)
    mid = rest.astype(BF16)
    low = (rest - mid.astype(F32)).astype(BF16)
    return high, mid, low


def moments_kernel(core_ref, x_ref, keep_ref, send_ref, tri_ref, sems):
    def put(tile, value):
        at = BLK * (tile % (TILES // 2))
        tri_ref[tile // (TILES // 2), at : at + BLK, :] = value

    x = x_ref[...]
    sums = nn(jnp.ones((8, x.shape[0]), BF16), x)
    put(
        TILES - 1,
        jnp.concatenate(
            [sums[:, LANES * j : LANES * (j + 1)] for j in range(FEAT // LANES)]
            + [jnp.zeros((BLK - 8 * (FEAT // LANES), LANES), F32)],
            axis=0,
        ),
    )
    halves = {}
    for b in range(FEAT // 256):
        left = x[:, 256 * b : 256 * (b + 1)].T
        wide = nn(left, x[:, : 256 * (b + 1)])
        for i in range(4 * b, 4 * b + 4):
            strip = wide[BLK * (i - 4 * b) : BLK * (i - 4 * b + 1), :]
            for j in range((i + 1) // 2):
                put(WHOLE.index((i, j)), strip[:, LANES * j : LANES * (j + 1)])
            if i % 2 == 0:
                halves[i] = strip[:, BLK * i : BLK * (i + 1)]
    for n, (i, j) in enumerate(PAIRED):
        put(len(WHOLE) + n, jnp.concatenate([halves[i], halves[j]], axis=1))
    core = core_ref[0]
    mine = pltpu.make_async_copy(tri_ref.at[core], keep_ref, sems.at[0])
    other = pltpu.make_async_copy(tri_ref.at[1 - core], send_ref, sems.at[1])
    other.start()
    mine.start()
    other.wait()
    mine.wait()


def moments(core, x):
    half = jax.ShapeDtypeStruct((HALF, LANES), F32)
    return pl.pallas_call(
        moments_kernel,
        out_shape=(half, half),
        in_specs=[SM, VM],
        out_specs=(ANY, ANY),
        scratch_shapes=[pltpu.VMEM((2, HALF, LANES), F32), pltpu.SemaphoreType.DMA((2,))],
        compiler_params=PARAMS,
        name="moments",
    )(core, x)


def pack_kernel(x_ref, cluster_ref, index_ref, rows_ref, slot_ref):
    count = x_ref.shape[0]
    slots = rows_ref.shape[0]
    owners = slots // CAP
    cluster = cluster_ref[...]
    owner = cluster // CL_OWN
    member = lax.broadcasted_iota(jnp.int32, (owners, count), 0) == jnp.broadcast_to(
        owner, (owners, count)
    )
    earlier = lax.broadcasted_iota(jnp.int32, (count, count), 0) < lax.broadcasted_iota(
        jnp.int32, (count, count), 1
    )
    prefix = nn(jnp.where(member, 1.0, 0.0).astype(BF16), jnp.where(earlier, 1.0, 0.0).astype(BF16))
    rank = jnp.sum(jnp.where(member, prefix, 0.0), axis=0, keepdims=True).astype(jnp.int32)
    slot = owner * CAP + rank
    slot_ref[...] = slot
    place = jnp.where(
        lax.broadcasted_iota(jnp.int32, (slots, count), 0) == jnp.broadcast_to(slot, (slots, count)),
        1.0,
        0.0,
    ).astype(BF16)
    rows_ref[:, :FEAT] = nn(place, x_ref[...]).astype(BF16)
    digit = lax.broadcasted_iota(jnp.int32, (LANES, count), 0)
    whole = jnp.broadcast_to(cluster * INDEX_SPAN + index_ref[...], (LANES, count))
    parts = jnp.where(digit < 4, (whole >> (7 * jnp.minimum(digit, 3))) & 127, 1)
    rows_ref[:, FEAT:] = nt(place, parts.astype(F32).astype(BF16)).astype(BF16)


def pack(x, cluster_id, row_index, owners):
    count = x.shape[0]
    slots = owners * CAP
    return pl.pallas_call(
        pack_kernel,
        out_shape=(
            jax.ShapeDtypeStruct((slots, WIDE), BF16),
            jax.ShapeDtypeStruct((1, count), jnp.int32),
        ),
        in_specs=[VM, VM, VM],
        out_specs=(VM, VM),
        compiler_params=PARAMS,
        name="pack_rows",
    )(x, cluster_id.reshape(1, count), row_index.reshape(1, count))


def inverse_factor(block, spot_ref):
    lane = lax.broadcasted_iota(jnp.int32, (8, LANES), 1)
    sub = lax.broadcasted_iota(jnp.int32, (8, LANES), 0)
    wide = jnp.concatenate([block, jnp.zeros((BLK, BLK), F32)], axis=1)
    a = [
        jnp.where(lane < BLK, wide[8 * g : 8 * g + 8], jnp.where(lane == sub + 8 * g + BLK, 1.0, 0.0))
        for g in range(PANELS)
    ]
    out = []

    def row(x, k):
        return jnp.broadcast_to(x[k : k + 1, :], (8, LANES))

    def column(x, k):
        return jnp.broadcast_to(x[:, k : k + 1], (8, LANES))

    for g in range(PANELS):
        d = [column(a[g], 8 * g + k) for k in range(8)]
        m = {h: [column(a[h], 8 * g + k) for k in range(8)] for h in range(g + 1, PANELS)}
        base = 64 * (g % 2)
        for l in range(8):
            spot_ref[base + 8 * l : base + 8 * l + 8, :] = d[l]
        s = {
            (k, l): jnp.broadcast_to(spot_ref[base + 8 * l + k : base + 8 * l + k + 1, :], (8, LANES))
            for k in range(8)
            for l in range(k, 8)
        }
        scale = [None] * 8
        for k in range(0, 8, 2):
            p, q, t = s[k, k], s[k, k + 1], s[k + 1, k + 1]
            det = p * t - q * q
            guess = pl.reciprocal(det, approx=True)
            fix = 2.0 - det * guess
            over = guess * fix
            ua = {l: s[k, l] * t - s[k + 1, l] * q for l in range(k + 2, 8)}
            ub = {l: s[k + 1, l] * p - s[k, l] * q for l in range(k + 2, 8)}
            for l in range(k + 2, 8):
                for n in range(l, 8):
                    num = ua[l] * s[k, n] + ub[l] * s[k + 1, n]
                    s[l, n] = s[l, n] - (num * guess) * fix
            root = lax.rsqrt(p)
            scale[k] = root
            scale[k + 1] = lax.rsqrt(det) * (p * root)
            a0, a1 = row(a[g], k), row(a[g], k + 1)
            va = (a0 * t - a1 * q) * over
            vb = (a1 * p - a0 * q) * over
            sa = {l: ua[l] * over for l in ua}
            sb = {l: ub[l] * over for l in ub}
            ma = jnp.where(sub > k + 1, d[k], 0.0)
            mb = jnp.where(sub > k + 1, d[k + 1], 0.0)
            for l in range(k + 2, 8):
                d[l] = d[l] - (ma * sa[l] + mb * sb[l])
            low = jnp.where(sub == k + 1, q * (root * root), 0.0)
            a[g] = a[g] - (ma * va + mb * vb) - low * a0
            for h in range(g + 1, PANELS):
                ha, hb = m[h][k], m[h][k + 1]
                for l in range(k + 2, 8):
                    m[h][l] = m[h][l] - (ha * sa[l] + hb * sb[l])
                a[h] = a[h] - (ha * va + hb * vb)
        scales = scale[0]
        for k in range(1, 8):
            scales = jnp.where(sub == k, scale[k], scales)
        out.append(a[g] * scales)
    return jnp.concatenate(out, axis=0)[:, BLK:]


def left6(x):
    high, mid, low = split3(x)
    return jnp.concatenate([high, high, mid, mid, high, low], axis=1)


def right6(x, axis):
    high, mid, low = split3(x)
    return jnp.concatenate([high, mid, high, mid, low, high], axis=axis)


def factor_kernel(total_rows, core_ref, mine_ref, other_ref, w_ref, mean_ref, s_ref, spot_ref):
    core = core_ref[0]

    def assemble(halves):
        def get(tile):
            at = BLK * (tile % (TILES // 2))
            return halves[tile // (TILES // 2)][at : at + BLK, :] * (1.0 / total_rows)

        sums = get(TILES - 1)
        means = [sums[8 * j : 8 * j + 1, :] for j in range(FEAT // LANES)]
        turned = sums.T

        def mean_column(i):
            return turned[BLK * (i % 2) : BLK * (i % 2 + 1), 8 * (i // 2) : 8 * (i // 2) + 1]

        for tile, (i, j) in enumerate(WHOLE):
            s_ref[BLK * i : BLK * (i + 1), LANES * j : LANES * (j + 1)] = (
                get(tile) - mean_column(i) * means[j]
            )
        for n, pair in enumerate(PAIRED):
            both = get(len(WHOLE) + n)
            for side, i in enumerate(pair):
                part = both[:, BLK * side : BLK * (side + 1)]
                s_ref[BLK * i : BLK * (i + 1), BLK * i : BLK * (i + 1)] = (
                    part - mean_column(i) * means[i // 2][:, :BLK]
                )
        parts = split3(jnp.concatenate(means, axis=1))
        mean_ref[...] = jnp.concatenate(
            [p.astype(F32) for p in parts] + [jnp.zeros((13, FEAT), F32)], axis=0
        ).astype(BF16)

    @pl.when(core == 0)
    def _():
        assemble((mine_ref, other_ref))

    @pl.when(core == 1)
    def _():
        assemble((other_ref, mine_ref))

    w_ref[...] = jnp.zeros((FEAT, FEAT), F32)

    def trailing(k, inv6):
        at, to = BLK * k, BLK * (k + 1)
        below = nt(left6(s_ref[to:, at:to]), inv6)
        left, right = left6(below), right6(below, 1)
        for begin in range(0, FEAT - to, 256):
            end = min(begin + 256, FEAT - to)
            skip = BLK if begin == 0 else begin
            if skip < end:
                s_ref[to + skip : to + end, to : to + end] = s_ref[
                    to + skip : to + end, to : to + end
                ] - nt(left[skip:end], right[:end])
        w_ref[to:, :to] = w_ref[to:, :to] - nn(left, right6(w_ref[at:to, :to], 0))

    waiting = None
    for k in range(NBLK):
        at, to = BLK * k, BLK * (k + 1)
        inv = inverse_factor(s_ref[at:to, at:to], spot_ref)
        if waiting is not None:
            trailing(*waiting)
        inv6 = right6(inv, 1)
        if to < FEAT:
            first = nt(left6(s_ref[to : to + BLK, at:to]), inv6)
            s_ref[to : to + BLK, to : to + BLK] = s_ref[to : to + BLK, to : to + BLK] - nt(
                left6(first), right6(first, 1)
            )
            waiting = (k, inv6)
        if k:
            w_ref[at:to, :at] = nn(left6(inv), right6(w_ref[at:to, :at], 0))
        w_ref[at:to, at:to] = inv


def best_kernel(rows_ref, w_ref, mean_ref, best_ref, x_ref, z_ref, u_ref, sems):
    slots = rows_ref.shape[0]
    piece = slots // PIECES
    copies = [
        pltpu.make_async_copy(
            rows_ref.at[piece * i : piece * (i + 1)], x_ref.at[piece * i : piece * (i + 1)], sems.at[i]
        )
        for i in range(PIECES)
    ]
    for copy in copies:
        copy.start()
    parts = [split3(w_ref[256 * n : 256 * (n + 1), : 256 * (n + 1)]) for n in range(FEAT // 256)]

    def whiten(x, n):
        high, mid, low = parts[n]
        x = x[:, : 256 * (n + 1)]
        return nt(x, low) + nt(x, mid) + nt(x, high)

    shift = [
        jnp.sum(whiten(mean_ref[...], n), axis=0, keepdims=True) for n in range(FEAT // 256)
    ]
    for i, copy in enumerate(copies):
        copy.wait()
        here = slice(piece * i, piece * (i + 1))
        x = x_ref[here, :FEAT]
        norm = jnp.zeros((piece, 1), F32)
        for n in range(FEAT // 256):
            z = whiten(x, n) - shift[n]
            norm = norm + jnp.sum(z * z, axis=1, keepdims=True)
            z_ref[here, 256 * n : 256 * (n + 1)] = z
        u_ref[here, :] = (z_ref[here, :] * lax.rsqrt(norm + 1e-06)).astype(BF16)

    digits = x_ref[:, FEAT:]
    lane = lax.broadcasted_iota(jnp.int32, (2 * LANES, LANES), 1)
    upper = lax.broadcasted_iota(jnp.int32, (2 * LANES, LANES), 0) >= LANES
    low_weight = jnp.where(lane == 0, 1.0, jnp.where(lane == 1, 128.0, 0.0))
    high_weight = jnp.where(
        lane == 2, 1.0, jnp.where(lane == 3, 128.0, jnp.where(lane == 4, -16384.0, 0.0))
    )
    weight = jnp.where(upper, high_weight, low_weight).astype(BF16)
    down = nt(digits, weight).astype(jnp.int32)
    kkey = down[:, :LANES] + ((down[:, LANES:] + 16384) << 14)
    across = nt(weight, digits).astype(jnp.int32)
    qkey = across[0:1] + ((across[LANES : LANES + 1] + 16384) << 14)
    floor = qkey & ~(INDEX_SPAN - 1)
    best = jnp.full((1, slots), -1.0, F32)
    rows = 256
    for b in range(slots // rows):
        scores = nt(u_ref[rows * b : rows * (b + 1), :], u_ref[...])
        keys = kkey[rows * b : rows * (b + 1), :]
        found = []
        for c in range(0, slots, LANES):
            to = c + LANES
            allowed = (keys < qkey[:, c:to]) & (keys >= floor[:, c:to])
            found.append(
                jnp.max(jnp.where(allowed, scores[:, c:to], -1.0), axis=0, keepdims=True)
            )
        best = jnp.maximum(best, jnp.concatenate(found, axis=1))
    for o in range(slots // CAP):
        best_ref[o : o + 1, :] = best[:, CAP * o : CAP * (o + 1)]


def factor(core, mine, other, total_rows):
    return pl.pallas_call(
        functools.partial(factor_kernel, total_rows),
        out_shape=(
            jax.ShapeDtypeStruct((FEAT, FEAT), F32),
            jax.ShapeDtypeStruct((16, FEAT), BF16),
        ),
        in_specs=[SM, VM, VM],
        out_specs=(VM, VM),
        scratch_shapes=[pltpu.VMEM((FEAT, FEAT), F32), pltpu.VMEM((128, LANES), F32)],
        compiler_params=PARAMS,
        name="factor",
    )(core, mine, other)


def best_of(rows, inverse, mean):
    slots = rows.shape[0]
    return pl.pallas_call(
        best_kernel,
        out_shape=jax.ShapeDtypeStruct((slots // CAP, CAP), F32),
        in_specs=[ANY, VM, VM],
        out_specs=VM,
        scratch_shapes=[
            pltpu.VMEM((slots, WIDE), BF16),
            pltpu.VMEM((slots, FEAT), F32),
            pltpu.VMEM((slots, FEAT), BF16),
            pltpu.SemaphoreType.DMA((PIECES,)),
        ],
        compiler_params=PARAMS,
        name="best",
    )(rows, inverse, mean)


def unpack_kernel(best_ref, slot_ref, out_ref):
    best = best_ref[...]
    owners = best.shape[0]
    count = slot_ref.shape[1]
    slot = slot_ref[...]
    rank = jnp.broadcast_to(slot % CAP, (CAP, count))
    pick = jnp.where(lax.broadcasted_iota(jnp.int32, (CAP, count), 0) == rank, 1.0, 0.0)
    table = nn(best, pick.astype(F32), HIGHEST)
    owner = jnp.broadcast_to(slot // CAP, (owners, count))
    mine = lax.broadcasted_iota(jnp.int32, (owners, count), 0) == owner
    out_ref[...] = jnp.sum(jnp.where(mine, table, 0.0), axis=0, keepdims=True)


def unpack(best, slot):
    return pl.pallas_call(
        unpack_kernel,
        out_shape=jax.ShapeDtypeStruct(slot.shape, F32),
        in_specs=[VM, VM],
        out_specs=VM,
        compiler_params=PARAMS,
        name="unpack",
    )(best, slot)


def exchange(x, axis):
    return lax.all_to_all(x, axis, split_axis=0, concat_axis=0, tiled=True)


def on_device(embeddings, cluster_id, row_index):
    count = embeddings.shape[0]
    across, deep, highs = lax.axis_size("x"), lax.axis_size("z"), lax.axis_size("y")
    owners = 2 * highs
    total_rows = count * owners * across * deep
    shard, plane = ("y", "core"), ("x", "y")
    swap = [(0, 1), (1, 0)]
    core = lax.axis_index("core").astype(jnp.int32).reshape(1)
    keep, send = moments(core, embeddings)
    pair = keep + lax.ppermute(send, "core", swap)
    shares = across * highs
    share = HALF // shares
    pair, embeddings = lax.optimization_barrier((pair, embeddings))
    spread = exchange(pair.reshape(shares, share, LANES), plane)
    packed, slot = pack(embeddings, cluster_id, row_index, owners)
    part = jnp.sum(spread, axis=0)
    part, packed = lax.optimization_barrier((part, packed))
    column = exchange(jnp.broadcast_to(part[None], (deep, share, LANES)), "z")
    total = jnp.sum(column, axis=0)
    mine = exchange(jnp.broadcast_to(total[None], (shares, share, LANES)), plane)
    mine = mine.reshape(HALF, LANES)
    rows = exchange(packed.reshape(owners, CAP, WIDE), shard).reshape(owners * CAP, WIDE)
    other = lax.ppermute(mine, "core", swap)
    inverse, mean = factor(core, mine, other, total_rows)
    best = best_of(rows, inverse, mean)
    returned = exchange(best, shard)
    return unpack(returned, slot).reshape(count)


def solution(mesh):
    groups, shards = mesh.devices.shape
    deep = min(16, groups)
    split = Mesh(
        mesh.devices.reshape(groups // deep, deep, shards // 2, 2), ("x", "z", "y", "core")
    )
    rows = ("x", "z", "y", "core")
    return jax.shard_map(
        on_device,
        mesh=split,
        in_specs=(P(rows, None), P(rows), P(rows)),
        out_specs=P(rows),
        check_vma=False,
    )
```

```python
import functools

import jax
import jax.numpy as jnp
from jax import lax
from jax.experimental import pallas as pl
from jax.experimental.pallas import tpu as pltpu
from jax.sharding import Mesh, PartitionSpec as P

F32 = jnp.float32
BF16 = jnp.bfloat16
FEAT = 768
BLK = 64
NBLK = FEAT // BLK
PANELS = BLK // 8
LANES = 128
WHOLE = [(i, j) for i in range(NBLK) for j in range((i + 1) // 2)]
PAIRED = [(i, i + 2) for i in range(0, NBLK, 4)]
TILES = len(WHOLE) + len(PAIRED) + 1
HALF = TILES // 2 * BLK
QUARTER = HALF // 4
WIDE = FEAT + LANES
CAP = 64
CL_OWN = 8
INDEX_SPAN = 2**19
PIECES = 2
DEEP = 16
HIGHEST = lax.Precision.HIGHEST
VM = pl.BlockSpec(memory_space=pltpu.VMEM)
SM = pl.BlockSpec(memory_space=pltpu.SMEM)
ANY = pl.BlockSpec(memory_space=pl.ANY)
HBM = pl.BlockSpec(memory_space=pltpu.HBM)
PARAMS = pltpu.CompilerParams(vmem_limit_bytes=24 * 2**20)


def nt(a, b, precision=None):
    return lax.dot_general(
        a, b, (((1,), (1,)), ((), ())), precision=precision, preferred_element_type=F32
    )


def nn(a, b, precision=None):
    return lax.dot_general(
        a, b, (((1,), (0,)), ((), ())), precision=precision, preferred_element_type=F32
    )


def split3(x):
    high = x.astype(BF16)
    rest = x - high.astype(F32)
    mid = rest.astype(BF16)
    low = (rest - mid.astype(F32)).astype(BF16)
    return high, mid, low


def moments_kernel(core_ref, x_ref, keep_ref, send_ref, tri_ref, sems):
    def put(tile, value):
        at = BLK * (tile % (TILES // 2))
        tri_ref[tile // (TILES // 2), at : at + BLK, :] = value

    x = x_ref[...]
    sums = nn(jnp.ones((8, x.shape[0]), BF16), x)
    put(
        TILES - 1,
        jnp.concatenate(
            [sums[:, LANES * j : LANES * (j + 1)] for j in range(FEAT // LANES)]
            + [jnp.zeros((BLK - 8 * (FEAT // LANES), LANES), F32)],
            axis=0,
        ),
    )
    halves = {}
    for b in range(FEAT // 256):
        left = x[:, 256 * b : 256 * (b + 1)].T
        wide = nn(left, x[:, : 256 * (b + 1)])
        for i in range(4 * b, 4 * b + 4):
            strip = wide[BLK * (i - 4 * b) : BLK * (i - 4 * b + 1), :]
            for j in range((i + 1) // 2):
                put(WHOLE.index((i, j)), strip[:, LANES * j : LANES * (j + 1)])
            if i % 2 == 0:
                halves[i] = strip[:, BLK * i : BLK * (i + 1)]
    for n, (i, j) in enumerate(PAIRED):
        put(len(WHOLE) + n, jnp.concatenate([halves[i], halves[j]], axis=1))
    core = core_ref[0]
    mine = pltpu.make_async_copy(tri_ref.at[core], keep_ref, sems.at[0])
    other = pltpu.make_async_copy(tri_ref.at[1 - core], send_ref, sems.at[1])
    other.start()
    mine.start()
    other.wait()
    mine.wait()


def moments(core, x):
    half = jax.ShapeDtypeStruct((HALF, LANES), F32)
    return pl.pallas_call(
        moments_kernel,
        out_shape=(half, half),
        in_specs=[SM, VM],
        out_specs=(ANY, ANY),
        scratch_shapes=[pltpu.VMEM((2, HALF, LANES), F32), pltpu.SemaphoreType.DMA((2,))],
        compiler_params=PARAMS,
        name="moments",
    )(core, x)


def pack_kernel(x_ref, cluster_ref, index_ref, rows_ref, slot_ref):
    count = x_ref.shape[0]
    slots = rows_ref.shape[0]
    owners = slots // CAP
    cluster = cluster_ref[...]
    owner = cluster // CL_OWN
    member = lax.broadcasted_iota(jnp.int32, (owners, count), 0) == jnp.broadcast_to(
        owner, (owners, count)
    )
    earlier = lax.broadcasted_iota(jnp.int32, (count, count), 0) < lax.broadcasted_iota(
        jnp.int32, (count, count), 1
    )
    prefix = nn(jnp.where(member, 1.0, 0.0).astype(BF16), jnp.where(earlier, 1.0, 0.0).astype(BF16))
    rank = jnp.sum(jnp.where(member, prefix, 0.0), axis=0, keepdims=True).astype(jnp.int32)
    slot = owner * CAP + rank
    slot_ref[...] = slot
    place = jnp.where(
        lax.broadcasted_iota(jnp.int32, (slots, count), 0) == jnp.broadcast_to(slot, (slots, count)),
        1.0,
        0.0,
    ).astype(BF16)
    rows_ref[:, :FEAT] = nn(place, x_ref[...]).astype(BF16)
    digit = lax.broadcasted_iota(jnp.int32, (LANES, count), 0)
    whole = jnp.broadcast_to(cluster * INDEX_SPAN + index_ref[...], (LANES, count))
    parts = jnp.where(digit < 4, (whole >> (7 * jnp.minimum(digit, 3))) & 127, 1)
    rows_ref[:, FEAT:] = nt(place, parts.astype(F32).astype(BF16)).astype(BF16)


def pack(x, cluster_id, row_index, owners):
    count = x.shape[0]
    slots = owners * CAP
    return pl.pallas_call(
        pack_kernel,
        out_shape=(
            jax.ShapeDtypeStruct((slots, WIDE), BF16),
            jax.ShapeDtypeStruct((1, count), jnp.int32),
        ),
        in_specs=[VM, VM, VM],
        out_specs=(VM, VM),
        compiler_params=PARAMS,
        name="pack_rows",
    )(x, cluster_id.reshape(1, count), row_index.reshape(1, count))


def inverse_factor(block, spot_ref):
    lane = lax.broadcasted_iota(jnp.int32, (8, LANES), 1)
    sub = lax.broadcasted_iota(jnp.int32, (8, LANES), 0)
    wide = jnp.concatenate([block, jnp.zeros((BLK, BLK), F32)], axis=1)
    a = [
        jnp.where(lane < BLK, wide[8 * g : 8 * g + 8], jnp.where(lane == sub + 8 * g + BLK, 1.0, 0.0))
        for g in range(PANELS)
    ]
    out = []

    def row(x, k):
        return jnp.broadcast_to(x[k : k + 1, :], (8, LANES))

    def column(x, k):
        return jnp.broadcast_to(x[:, k : k + 1], (8, LANES))

    for g in range(PANELS):
        d = [column(a[g], 8 * g + k) for k in range(8)]
        m = {h: [column(a[h], 8 * g + k) for k in range(8)] for h in range(g + 1, PANELS)}
        base = 64 * (g % 2)
        for l in range(8):
            spot_ref[base + 8 * l : base + 8 * l + 8, :] = d[l]
        s = {
            (k, l): jnp.broadcast_to(spot_ref[base + 8 * l + k : base + 8 * l + k + 1, :], (8, LANES))
            for k in range(8)
            for l in range(k, 8)
        }
        scale = [None] * 8
        for k in range(0, 8, 2):
            p, q, t = s[k, k], s[k, k + 1], s[k + 1, k + 1]
            det = p * t - q * q
            over = pl.reciprocal(det, approx=True)
            ua = {l: s[k, l] * t - s[k + 1, l] * q for l in range(k + 2, 8)}
            ub = {l: s[k + 1, l] * p - s[k, l] * q for l in range(k + 2, 8)}
            for l in range(k + 2, 8):
                for n in range(l, 8):
                    num = ua[l] * s[k, n] + ub[l] * s[k + 1, n]
                    s[l, n] = s[l, n] - num * over
            root = lax.rsqrt(p)
            scale[k] = root
            scale[k + 1] = lax.rsqrt(det) * (p * root)
            a0, a1 = row(a[g], k), row(a[g], k + 1)
            va = (a0 * t - a1 * q) * over
            vb = (a1 * p - a0 * q) * over
            sa = {l: ua[l] * over for l in ua}
            sb = {l: ub[l] * over for l in ub}
            ma = jnp.where(sub > k + 1, d[k], 0.0)
            mb = jnp.where(sub > k + 1, d[k + 1], 0.0)
            for l in range(k + 2, 8):
                d[l] = d[l] - (ma * sa[l] + mb * sb[l])
            low = jnp.where(sub == k + 1, q * (root * root), 0.0)
            a[g] = a[g] - (ma * va + mb * vb) - low * a0
            for h in range(g + 1, PANELS):
                ha, hb = m[h][k], m[h][k + 1]
                for l in range(k + 2, 8):
                    m[h][l] = m[h][l] - (ha * sa[l] + hb * sb[l])
                a[h] = a[h] - (ha * va + hb * vb)
        scales = scale[0]
        for k in range(1, 8):
            scales = jnp.where(sub == k, scale[k], scales)
        out.append(a[g] * scales)
    return jnp.concatenate(out, axis=0)[:, BLK:]


def left6(x):
    high, mid, low = split3(x)
    return jnp.concatenate([high, high, mid, mid, high, low], axis=1)


def right6(x, axis):
    high, mid, low = split3(x)
    return jnp.concatenate([high, mid, high, mid, low, high], axis=axis)


def factor_kernel(
    total_rows, place_ref, near_ref, far_ref, near2_ref, far2_ref, out_ref, mean_ref, tri_ref, s_ref, w_ref, spot_ref, sems
):
    core, column = place_ref[0], place_ref[1]
    copies = []
    for side, parts in ((core, (near_ref, far_ref)), (1 - core, (near2_ref, far2_ref))):
        spot = 0
        for part in parts:
            for at in range(0, part.shape[0], QUARTER):
                piece = column ^ (spot ^ (spot >> 1))
                copies.append(
                    pltpu.make_async_copy(
                        part.at[at : at + QUARTER],
                        tri_ref.at[side, pl.ds(pl.multiple_of(piece * QUARTER, QUARTER), QUARTER)],
                        sems.at[len(copies)],
                    )
                )
                spot += 1
    for copy in copies:
        copy.start()
    for copy in copies:
        copy.wait()

    def get(tile):
        at = BLK * (tile % (TILES // 2))
        return tri_ref[tile // (TILES // 2), at : at + BLK, :] * (1.0 / total_rows)

    sums = get(TILES - 1)
    means = [sums[8 * j : 8 * j + 1, :] for j in range(FEAT // LANES)]
    turned = sums.T

    def mean_column(i):
        return turned[BLK * (i % 2) : BLK * (i % 2 + 1), 8 * (i // 2) : 8 * (i // 2) + 1]

    for tile, (i, j) in enumerate(WHOLE):
        s_ref[BLK * i : BLK * (i + 1), LANES * j : LANES * (j + 1)] = (
            get(tile) - mean_column(i) * means[j]
        )
    for n, pair in enumerate(PAIRED):
        both = get(len(WHOLE) + n)
        for side, i in enumerate(pair):
            part = both[:, BLK * side : BLK * (side + 1)]
            s_ref[BLK * i : BLK * (i + 1), BLK * i : BLK * (i + 1)] = (
                part - mean_column(i) * means[i // 2][:, :BLK]
            )
    parts = split3(jnp.concatenate(means, axis=1))
    mean_ref[...] = jnp.concatenate(
        [p.astype(F32) for p in parts] + [jnp.zeros((13, FEAT), F32)], axis=0
    ).astype(BF16)

    w_ref[...] = jnp.zeros((FEAT, FEAT), F32)

    def trailing(k, inv6):
        at, to = BLK * k, BLK * (k + 1)
        below = nt(left6(s_ref[to:, at:to]), inv6)
        left, right = left6(below), right6(below, 1)
        for begin in range(0, FEAT - to, 256):
            end = min(begin + 256, FEAT - to)
            skip = BLK if begin == 0 else begin
            if skip < end:
                s_ref[to + skip : to + end, to : to + end] = s_ref[
                    to + skip : to + end, to : to + end
                ] - nt(left[skip:end], right[:end])
        w_ref[to:, :to] = w_ref[to:, :to] - nn(left, right6(w_ref[at:to, :to], 0))

    waiting = None
    leaving = []
    for k in range(NBLK):
        at, to = BLK * k, BLK * (k + 1)
        inv = inverse_factor(s_ref[at:to, at:to], spot_ref)
        if waiting is not None:
            trailing(*waiting)
        inv6 = right6(inv, 1)
        if to < FEAT:
            first = nt(left6(s_ref[to : to + BLK, at:to]), inv6)
            s_ref[to : to + BLK, to : to + BLK] = s_ref[to : to + BLK, to : to + BLK] - nt(
                left6(first), right6(first, 1)
            )
            waiting = (k, inv6)
        if k:
            w_ref[at:to, :at] = nn(left6(inv), right6(w_ref[at:to, :at], 0))
        w_ref[at:to, at:to] = inv
        if to % 256 == 0:
            copy = pltpu.make_async_copy(
                w_ref.at[to - 256 : to, 0:to], out_ref.at[to - 256 : to, 0:to], sems.at[to // 256 - 1]
            )
            copy.start()
            leaving.append(copy)
    for copy in leaving:
        copy.wait()


def best_kernel(rows_ref, inverse_ref, mean_ref, best_ref, w_ref, x_ref, z_ref, u_ref, sems):
    slots = rows_ref.shape[0]
    piece = slots // PIECES
    copies = [
        pltpu.make_async_copy(
            rows_ref.at[piece * i : piece * (i + 1)], x_ref.at[piece * i : piece * (i + 1)], sems.at[i]
        )
        for i in range(PIECES)
    ]
    fetch = [
        pltpu.make_async_copy(
            inverse_ref.at[256 * n : 256 * (n + 1), 0 : 256 * (n + 1)],
            w_ref.at[256 * n : 256 * (n + 1), 0 : 256 * (n + 1)],
            sems.at[PIECES + n],
        )
        for n in range(FEAT // 256)
    ]
    for copy in fetch + copies:
        copy.start()
    parts = []
    for n in range(FEAT // 256):
        fetch[n].wait()
        parts.append(split3(w_ref[256 * n : 256 * (n + 1), : 256 * (n + 1)]))

    def whiten(x, n):
        high, mid, low = parts[n]
        x = x[:, : 256 * (n + 1)]
        return nt(x, low) + nt(x, mid) + nt(x, high)

    shift = [
        jnp.sum(whiten(mean_ref[...], n), axis=0, keepdims=True) for n in range(FEAT // 256)
    ]
    for i, copy in enumerate(copies):
        copy.wait()
        here = slice(piece * i, piece * (i + 1))
        x = x_ref[here, :FEAT]
        norm = jnp.zeros((piece, 1), F32)
        for n in range(FEAT // 256):
            z = whiten(x, n) - shift[n]
            norm = norm + jnp.sum(z * z, axis=1, keepdims=True)
            z_ref[here, 256 * n : 256 * (n + 1)] = z
        u_ref[here, :] = (z_ref[here, :] * lax.rsqrt(norm + 1e-06)).astype(BF16)

    digits = x_ref[:, FEAT:]
    lane = lax.broadcasted_iota(jnp.int32, (2 * LANES, LANES), 1)
    upper = lax.broadcasted_iota(jnp.int32, (2 * LANES, LANES), 0) >= LANES
    low_weight = jnp.where(lane == 0, 1.0, jnp.where(lane == 1, 128.0, 0.0))
    high_weight = jnp.where(
        lane == 2, 1.0, jnp.where(lane == 3, 128.0, jnp.where(lane == 4, -16384.0, 0.0))
    )
    weight = jnp.where(upper, high_weight, low_weight).astype(BF16)
    down = nt(digits, weight).astype(jnp.int32)
    kkey = down[:, :LANES] + ((down[:, LANES:] + 16384) << 14)
    across = nt(weight, digits).astype(jnp.int32)
    qkey = across[0:1] + ((across[LANES : LANES + 1] + 16384) << 14)
    floor = qkey & ~(INDEX_SPAN - 1)
    best = jnp.full((1, slots), -1.0, F32)
    rows = 256
    for b in range(slots // rows):
        scores = nt(u_ref[rows * b : rows * (b + 1), :], u_ref[...])
        keys = kkey[rows * b : rows * (b + 1), :]
        found = []
        for c in range(0, slots, LANES):
            to = c + LANES
            allowed = (keys < qkey[:, c:to]) & (keys >= floor[:, c:to])
            found.append(
                jnp.max(jnp.where(allowed, scores[:, c:to], -1.0), axis=0, keepdims=True)
            )
        best = jnp.maximum(best, jnp.concatenate(found, axis=1))
    for o in range(slots // CAP):
        best_ref[o : o + 1, :] = best[:, CAP * o : CAP * (o + 1)]


def factor(place, pieces, total_rows):
    return pl.pallas_call(
        functools.partial(factor_kernel, total_rows),
        out_shape=(
            jax.ShapeDtypeStruct((FEAT, FEAT), F32),
            jax.ShapeDtypeStruct((16, FEAT), BF16),
        ),
        in_specs=[SM, ANY, ANY, ANY, ANY],
        out_specs=(HBM, VM),
        scratch_shapes=[
            pltpu.VMEM((2, HALF, LANES), F32),
            pltpu.VMEM((FEAT, FEAT), F32),
            pltpu.VMEM((FEAT, FEAT), F32),
            pltpu.VMEM((128, LANES), F32),
            pltpu.SemaphoreType.DMA((8,)),
        ],
        compiler_params=PARAMS,
        name="factor",
    )(place, *pieces)


def best_of(rows, inverse, mean):
    slots = rows.shape[0]
    return pl.pallas_call(
        best_kernel,
        out_shape=jax.ShapeDtypeStruct((slots // CAP, CAP), F32),
        in_specs=[HBM, HBM, VM],
        out_specs=VM,
        scratch_shapes=[
            pltpu.VMEM((FEAT, FEAT), F32),
            pltpu.VMEM((slots, WIDE), BF16),
            pltpu.VMEM((slots, FEAT), F32),
            pltpu.VMEM((slots, FEAT), BF16),
            pltpu.SemaphoreType.DMA((PIECES + FEAT // 256,)),
        ],
        compiler_params=PARAMS,
        name="best",
    )(rows, inverse, mean)


def unpack_kernel(best_ref, slot_ref, out_ref):
    best = best_ref[...]
    owners = best.shape[0]
    count = slot_ref.shape[1]
    slot = slot_ref[...]
    rank = jnp.broadcast_to(slot % CAP, (CAP, count))
    pick = jnp.where(lax.broadcasted_iota(jnp.int32, (CAP, count), 0) == rank, 1.0, 0.0)
    table = nn(best, pick.astype(F32), HIGHEST)
    owner = jnp.broadcast_to(slot // CAP, (owners, count))
    mine = lax.broadcasted_iota(jnp.int32, (owners, count), 0) == owner
    out_ref[...] = jnp.sum(jnp.where(mine, table, 0.0), axis=0, keepdims=True)


def unpack(best, slot):
    return pl.pallas_call(
        unpack_kernel,
        out_shape=jax.ShapeDtypeStruct(slot.shape, F32),
        in_specs=[VM, VM],
        out_specs=VM,
        compiler_params=PARAMS,
        name="unpack",
    )(best, slot)


def exchange(x, axis):
    return lax.all_to_all(x, axis, split_axis=0, concat_axis=0, tiled=True)


def on_device(embeddings, cluster_id, row_index):
    count = embeddings.shape[0]
    across, deep, highs = lax.axis_size("x"), lax.axis_size("z"), lax.axis_size("y")
    owners = 2 * highs
    total_rows = count * owners * across * deep
    shard, plane = ("y", "core"), ("x", "y")
    swap = [(0, 1), (1, 0)]
    core = lax.axis_index("core").astype(jnp.int32)
    column = lax.axis_index("x").astype(jnp.int32)
    keep, send = moments(core.reshape(1), embeddings)
    pair = keep + lax.ppermute(send, "core", swap)
    shares = across * highs
    share = HALF // shares
    pair, embeddings = lax.optimization_barrier((pair, embeddings))
    spread = exchange(pair.reshape(shares, share, LANES), plane)
    packed, slot = pack(embeddings, cluster_id, row_index, owners)
    part = jnp.sum(spread, axis=0)
    part, packed = lax.optimization_barrier((part, packed))
    total = jnp.sum(exchange(jnp.broadcast_to(part[None], (deep, share, LANES)), "z"), axis=0)
    quarter = exchange(jnp.broadcast_to(total[None], (highs, share, LANES)), "y")
    quarter = quarter.reshape(highs * share, LANES)
    rows = exchange(packed.reshape(owners, CAP, WIDE), shard).reshape(owners * CAP, WIDE)
    beside = lax.ppermute(quarter, "x", [(i, i ^ 1) for i in range(across)])
    near = jnp.concatenate([quarter, beside], axis=0)
    far = lax.ppermute(near, "x", [(i, i ^ 3) for i in range(across)])
    near2 = lax.ppermute(near, "core", swap)
    far2 = lax.ppermute(far, "core", swap)
    place = jnp.stack([core, column])
    inverse, mean = factor(place, (near, far, near2, far2), total_rows)
    best = best_of(rows, inverse, mean)
    returned = exchange(best, shard)
    return unpack(returned, slot).reshape(count)


def solution(mesh):
    groups, shards = mesh.devices.shape
    deep = min(DEEP, groups)
    split = Mesh(
        mesh.devices.reshape(groups // deep, deep, shards // 2, 2), ("x", "z", "y", "core")
    )
    rows = ("x", "z", "y", "core")
    return jax.shard_map(
        on_device,
        mesh=split,
        in_specs=(P(rows, None), P(rows), P(rows)),
        out_specs=P(rows),
        check_vma=False,
    )
```

```python
import functools

import jax
import jax.numpy as jnp
from jax import lax
from jax.experimental import pallas as pl
from jax.experimental.pallas import tpu as pltpu
from jax.sharding import Mesh, PartitionSpec as P

F32 = jnp.float32
BF16 = jnp.bfloat16
FEAT = 768
BLK = 64
NBLK = FEAT // BLK
PANELS = BLK // 8
LANES = 128
WHOLE = [(i, j) for i in range(NBLK) for j in range((i + 1) // 2)]
PAIRED = [(i, i + 2) for i in range(0, NBLK, 4)]
TILES = len(WHOLE) + len(PAIRED) + 1
HALF = TILES // 2 * BLK
PART = HALF // 2
WIDE = FEAT + LANES
CAP = 64
CL_OWN = 8
INDEX_SPAN = 2**19
PIECES = 2
AXES = ("x_hi", "x_lo", "z_hi", "z_lo", "y", "core")
GROUP_SPLIT = (2, 2, 8, 2)
HIGHEST = lax.Precision.HIGHEST
VM = pl.BlockSpec(memory_space=pltpu.VMEM)
SM = pl.BlockSpec(memory_space=pltpu.SMEM)
ANY = pl.BlockSpec(memory_space=pl.ANY)
HBM = pl.BlockSpec(memory_space=pltpu.HBM)
PARAMS = pltpu.CompilerParams(vmem_limit_bytes=24 * 2**20)


def nt(a, b, precision=None):
    return lax.dot_general(
        a, b, (((1,), (1,)), ((), ())), precision=precision, preferred_element_type=F32
    )


def nn(a, b, precision=None):
    return lax.dot_general(
        a, b, (((1,), (0,)), ((), ())), precision=precision, preferred_element_type=F32
    )


def split3(x):
    high = x.astype(BF16)
    rest = x - high.astype(F32)
    mid = rest.astype(BF16)
    low = (rest - mid.astype(F32)).astype(BF16)
    return high, mid, low


def moments_kernel(core_ref, x_ref, keep_ref, send_ref, tri_ref, sems):
    def put(tile, value):
        at = BLK * (tile % (TILES // 2))
        tri_ref[tile // (TILES // 2), at : at + BLK, :] = value

    x = x_ref[...]
    sums = nn(jnp.ones((8, x.shape[0]), BF16), x)
    put(
        TILES - 1,
        jnp.concatenate(
            [sums[:, LANES * j : LANES * (j + 1)] for j in range(FEAT // LANES)]
            + [jnp.zeros((BLK - 8 * (FEAT // LANES), LANES), F32)],
            axis=0,
        ),
    )
    halves = {}
    for b in range(FEAT // 256):
        left = x[:, 256 * b : 256 * (b + 1)].T
        wide = nn(left, x[:, : 256 * (b + 1)])
        for i in range(4 * b, 4 * b + 4):
            strip = wide[BLK * (i - 4 * b) : BLK * (i - 4 * b + 1), :]
            for j in range((i + 1) // 2):
                put(WHOLE.index((i, j)), strip[:, LANES * j : LANES * (j + 1)])
            if i % 2 == 0:
                halves[i] = strip[:, BLK * i : BLK * (i + 1)]
    for n, (i, j) in enumerate(PAIRED):
        put(len(WHOLE) + n, jnp.concatenate([halves[i], halves[j]], axis=1))
    core = core_ref[0]
    mine = pltpu.make_async_copy(tri_ref.at[core], keep_ref, sems.at[0])
    other = pltpu.make_async_copy(tri_ref.at[1 - core], send_ref, sems.at[1])
    other.start()
    mine.start()
    other.wait()
    mine.wait()


def moments(core, x):
    half = jax.ShapeDtypeStruct((HALF, LANES), F32)
    return pl.pallas_call(
        moments_kernel,
        out_shape=(half, half),
        in_specs=[SM, VM],
        out_specs=(ANY, ANY),
        scratch_shapes=[pltpu.VMEM((2, HALF, LANES), F32), pltpu.SemaphoreType.DMA((2,))],
        compiler_params=PARAMS,
        name="moments",
    )(core, x)


def pack_kernel(x_ref, cluster_ref, index_ref, rows_ref, slot_ref):
    count = x_ref.shape[0]
    slots = rows_ref.shape[0]
    owners = slots // CAP
    cluster = cluster_ref[...]
    owner = cluster // CL_OWN
    member = lax.broadcasted_iota(jnp.int32, (owners, count), 0) == jnp.broadcast_to(
        owner, (owners, count)
    )
    earlier = lax.broadcasted_iota(jnp.int32, (count, count), 0) < lax.broadcasted_iota(
        jnp.int32, (count, count), 1
    )
    prefix = nn(jnp.where(member, 1.0, 0.0).astype(BF16), jnp.where(earlier, 1.0, 0.0).astype(BF16))
    rank = jnp.sum(jnp.where(member, prefix, 0.0), axis=0, keepdims=True).astype(jnp.int32)
    slot = owner * CAP + rank
    slot_ref[...] = slot
    place = jnp.where(
        lax.broadcasted_iota(jnp.int32, (slots, count), 0) == jnp.broadcast_to(slot, (slots, count)),
        1.0,
        0.0,
    ).astype(BF16)
    rows_ref[:, :FEAT] = nn(place, x_ref[...]).astype(BF16)
    digit = lax.broadcasted_iota(jnp.int32, (LANES, count), 0)
    whole = jnp.broadcast_to(cluster * INDEX_SPAN + index_ref[...], (LANES, count))
    parts = jnp.where(digit < 4, (whole >> (7 * jnp.minimum(digit, 3))) & 127, 1)
    rows_ref[:, FEAT:] = nt(place, parts.astype(F32).astype(BF16)).astype(BF16)


def pack(x, cluster_id, row_index, owners):
    count = x.shape[0]
    slots = owners * CAP
    return pl.pallas_call(
        pack_kernel,
        out_shape=(
            jax.ShapeDtypeStruct((slots, WIDE), BF16),
            jax.ShapeDtypeStruct((1, count), jnp.int32),
        ),
        in_specs=[VM, VM, VM],
        out_specs=(VM, VM),
        compiler_params=PARAMS,
        name="pack_rows",
    )(x, cluster_id.reshape(1, count), row_index.reshape(1, count))


def inverse_factor(block, spot_ref):
    lane = lax.broadcasted_iota(jnp.int32, (8, LANES), 1)
    sub = lax.broadcasted_iota(jnp.int32, (8, LANES), 0)
    wide = jnp.concatenate([block, jnp.zeros((BLK, BLK), F32)], axis=1)
    a = [
        jnp.where(lane < BLK, wide[8 * g : 8 * g + 8], jnp.where(lane == sub + 8 * g + BLK, 1.0, 0.0))
        for g in range(PANELS)
    ]
    out = []

    def row(x, k):
        return jnp.broadcast_to(x[k : k + 1, :], (8, LANES))

    def column(x, k):
        return jnp.broadcast_to(x[:, k : k + 1], (8, LANES))

    for g in range(PANELS):
        d = [column(a[g], 8 * g + k) for k in range(8)]
        m = {h: [column(a[h], 8 * g + k) for k in range(8)] for h in range(g + 1, PANELS)}
        base = 64 * (g % 2)
        for l in range(8):
            spot_ref[base + 8 * l : base + 8 * l + 8, :] = d[l]
        s = {
            (k, l): jnp.broadcast_to(spot_ref[base + 8 * l + k : base + 8 * l + k + 1, :], (8, LANES))
            for k in range(8)
            for l in range(k, 8)
        }
        scale = [None] * 8
        for k in range(0, 8, 2):
            p, q, t = s[k, k], s[k, k + 1], s[k + 1, k + 1]
            det = p * t - q * q
            over = pl.reciprocal(det, approx=True)
            ua = {l: s[k, l] * t - s[k + 1, l] * q for l in range(k + 2, 8)}
            ub = {l: s[k + 1, l] * p - s[k, l] * q for l in range(k + 2, 8)}
            for l in range(k + 2, 8):
                for n in range(l, 8):
                    num = ua[l] * s[k, n] + ub[l] * s[k + 1, n]
                    s[l, n] = s[l, n] - num * over
            root = lax.rsqrt(p)
            scale[k] = root
            scale[k + 1] = lax.rsqrt(det) * (p * root)
            a0, a1 = row(a[g], k), row(a[g], k + 1)
            va = (a0 * t - a1 * q) * over
            vb = (a1 * p - a0 * q) * over
            sa = {l: ua[l] * over for l in ua}
            sb = {l: ub[l] * over for l in ub}
            ma = jnp.where(sub > k + 1, d[k], 0.0)
            mb = jnp.where(sub > k + 1, d[k + 1], 0.0)
            for l in range(k + 2, 8):
                d[l] = d[l] - (ma * sa[l] + mb * sb[l])
            low = jnp.where(sub == k + 1, q * (root * root), 0.0)
            a[g] = a[g] - (ma * va + mb * vb) - low * a0
            for h in range(g + 1, PANELS):
                ha, hb = m[h][k], m[h][k + 1]
                for l in range(k + 2, 8):
                    m[h][l] = m[h][l] - (ha * sa[l] + hb * sb[l])
                a[h] = a[h] - (ha * va + hb * vb)
        scales = scale[0]
        for k in range(1, 8):
            scales = jnp.where(sub == k, scale[k], scales)
        out.append(a[g] * scales)
    return jnp.concatenate(out, axis=0)[:, BLK:]


def left6(x):
    high, mid, low = split3(x)
    return jnp.concatenate([high, high, mid, mid, high, low], axis=1)


def right6(x, axis):
    high, mid, low = split3(x)
    return jnp.concatenate([high, mid, high, mid, low, high], axis=axis)


def factor_kernel(
    total_rows, place_ref, near_ref, far_ref, near2_ref, far2_ref, out_ref, mean_ref, tri_ref, s_ref, w_ref, spot_ref, sems
):
    core, half = place_ref[0], place_ref[1]
    copies = []
    for side, parts in ((core, (near_ref, far_ref)), (1 - core, (near2_ref, far2_ref))):
        for part, spot in zip(parts, (half, 1 - half)):
            copies.append(
                pltpu.make_async_copy(
                    part, tri_ref.at[side, pl.ds(pl.multiple_of(spot * PART, PART), PART)], sems.at[len(copies)]
                )
            )
    for copy in copies:
        copy.start()
    for copy in copies:
        copy.wait()

    def get(tile):
        at = BLK * (tile % (TILES // 2))
        return tri_ref[tile // (TILES // 2), at : at + BLK, :] * (1.0 / total_rows)

    sums = get(TILES - 1)
    means = [sums[8 * j : 8 * j + 1, :] for j in range(FEAT // LANES)]
    turned = sums.T

    def mean_column(i):
        return turned[BLK * (i % 2) : BLK * (i % 2 + 1), 8 * (i // 2) : 8 * (i // 2) + 1]

    for tile, (i, j) in enumerate(WHOLE):
        s_ref[BLK * i : BLK * (i + 1), LANES * j : LANES * (j + 1)] = (
            get(tile) - mean_column(i) * means[j]
        )
    for n, pair in enumerate(PAIRED):
        both = get(len(WHOLE) + n)
        for side, i in enumerate(pair):
            part = both[:, BLK * side : BLK * (side + 1)]
            s_ref[BLK * i : BLK * (i + 1), BLK * i : BLK * (i + 1)] = (
                part - mean_column(i) * means[i // 2][:, :BLK]
            )
    parts = split3(jnp.concatenate(means, axis=1))
    mean_ref[...] = jnp.concatenate(
        [p.astype(F32) for p in parts] + [jnp.zeros((13, FEAT), F32)], axis=0
    ).astype(BF16)

    w_ref[...] = jnp.zeros((FEAT, FEAT), F32)

    def trailing(k, inv6):
        at, to = BLK * k, BLK * (k + 1)
        below = nt(left6(s_ref[to:, at:to]), inv6)
        left, right = left6(below), right6(below, 1)
        for begin in range(0, FEAT - to, 256):
            end = min(begin + 256, FEAT - to)
            skip = BLK if begin == 0 else begin
            if skip < end:
                s_ref[to + skip : to + end, to : to + end] = s_ref[
                    to + skip : to + end, to : to + end
                ] - nt(left[skip:end], right[:end])
        w_ref[to:, :to] = w_ref[to:, :to] - nn(left, right6(w_ref[at:to, :to], 0))

    waiting = None
    leaving = []
    for k in range(NBLK):
        at, to = BLK * k, BLK * (k + 1)
        inv = inverse_factor(s_ref[at:to, at:to], spot_ref)
        if waiting is not None:
            trailing(*waiting)
        inv6 = right6(inv, 1)
        if to < FEAT:
            first = nt(left6(s_ref[to : to + BLK, at:to]), inv6)
            s_ref[to : to + BLK, to : to + BLK] = s_ref[to : to + BLK, to : to + BLK] - nt(
                left6(first), right6(first, 1)
            )
            waiting = (k, inv6)
        if k:
            w_ref[at:to, :at] = nn(left6(inv), right6(w_ref[at:to, :at], 0))
        w_ref[at:to, at:to] = inv
        if to % 256 == 0:
            copy = pltpu.make_async_copy(
                w_ref.at[to - 256 : to, 0:to], out_ref.at[to - 256 : to, 0:to], sems.at[to // 256 - 1]
            )
            copy.start()
            leaving.append(copy)
    for copy in leaving:
        copy.wait()


def best_kernel(rows_ref, inverse_ref, mean_ref, best_ref, w_ref, x_ref, z_ref, u_ref, sems):
    slots = rows_ref.shape[0]
    piece = slots // PIECES
    copies = [
        pltpu.make_async_copy(
            rows_ref.at[piece * i : piece * (i + 1)], x_ref.at[piece * i : piece * (i + 1)], sems.at[i]
        )
        for i in range(PIECES)
    ]
    fetch = [
        pltpu.make_async_copy(
            inverse_ref.at[256 * n : 256 * (n + 1), 0 : 256 * (n + 1)],
            w_ref.at[256 * n : 256 * (n + 1), 0 : 256 * (n + 1)],
            sems.at[PIECES + n],
        )
        for n in range(FEAT // 256)
    ]
    for copy in fetch + copies:
        copy.start()
    parts = []
    for n in range(FEAT // 256):
        fetch[n].wait()
        parts.append(split3(w_ref[256 * n : 256 * (n + 1), : 256 * (n + 1)]))

    def whiten(x, n):
        high, mid, low = parts[n]
        x = x[:, : 256 * (n + 1)]
        return nt(x, low) + nt(x, mid) + nt(x, high)

    shift = [
        jnp.sum(whiten(mean_ref[...], n), axis=0, keepdims=True) for n in range(FEAT // 256)
    ]
    for i, copy in enumerate(copies):
        copy.wait()
        here = slice(piece * i, piece * (i + 1))
        x = x_ref[here, :FEAT]
        norm = jnp.zeros((piece, 1), F32)
        for n in range(FEAT // 256):
            z = whiten(x, n) - shift[n]
            norm = norm + jnp.sum(z * z, axis=1, keepdims=True)
            z_ref[here, 256 * n : 256 * (n + 1)] = z
        u_ref[here, :] = (z_ref[here, :] * lax.rsqrt(norm + 1e-06)).astype(BF16)

    digits = x_ref[:, FEAT:]
    lane = lax.broadcasted_iota(jnp.int32, (2 * LANES, LANES), 1)
    upper = lax.broadcasted_iota(jnp.int32, (2 * LANES, LANES), 0) >= LANES
    low_weight = jnp.where(lane == 0, 1.0, jnp.where(lane == 1, 128.0, 0.0))
    high_weight = jnp.where(
        lane == 2, 1.0, jnp.where(lane == 3, 128.0, jnp.where(lane == 4, -16384.0, 0.0))
    )
    weight = jnp.where(upper, high_weight, low_weight).astype(BF16)
    down = nt(digits, weight).astype(jnp.int32)
    kkey = down[:, :LANES] + ((down[:, LANES:] + 16384) << 14)
    across = nt(weight, digits).astype(jnp.int32)
    qkey = across[0:1] + ((across[LANES : LANES + 1] + 16384) << 14)
    floor = qkey & ~(INDEX_SPAN - 1)
    best = jnp.full((1, slots), -1.0, F32)
    rows = 256
    for b in range(slots // rows):
        scores = nt(u_ref[rows * b : rows * (b + 1), :], u_ref[...])
        keys = kkey[rows * b : rows * (b + 1), :]
        found = []
        for c in range(0, slots, LANES):
            to = c + LANES
            allowed = (keys < qkey[:, c:to]) & (keys >= floor[:, c:to])
            found.append(
                jnp.max(jnp.where(allowed, scores[:, c:to], -1.0), axis=0, keepdims=True)
            )
        best = jnp.maximum(best, jnp.concatenate(found, axis=1))
    for o in range(slots // CAP):
        best_ref[o : o + 1, :] = best[:, CAP * o : CAP * (o + 1)]


def factor(place, pieces, total_rows):
    return pl.pallas_call(
        functools.partial(factor_kernel, total_rows),
        out_shape=(
            jax.ShapeDtypeStruct((FEAT, FEAT), F32),
            jax.ShapeDtypeStruct((16, FEAT), BF16),
        ),
        in_specs=[SM, ANY, ANY, ANY, ANY],
        out_specs=(HBM, VM),
        scratch_shapes=[
            pltpu.VMEM((2, HALF, LANES), F32),
            pltpu.VMEM((FEAT, FEAT), F32),
            pltpu.VMEM((FEAT, FEAT), F32),
            pltpu.VMEM((128, LANES), F32),
            pltpu.SemaphoreType.DMA((4,)),
        ],
        compiler_params=PARAMS,
        name="factor",
    )(place, *pieces)


def best_of(rows, inverse, mean):
    slots = rows.shape[0]
    return pl.pallas_call(
        best_kernel,
        out_shape=jax.ShapeDtypeStruct((slots // CAP, CAP), F32),
        in_specs=[HBM, HBM, VM],
        out_specs=VM,
        scratch_shapes=[
            pltpu.VMEM((FEAT, FEAT), F32),
            pltpu.VMEM((slots, WIDE), BF16),
            pltpu.VMEM((slots, FEAT), F32),
            pltpu.VMEM((slots, FEAT), BF16),
            pltpu.SemaphoreType.DMA((PIECES + FEAT // 256,)),
        ],
        compiler_params=PARAMS,
        name="best",
    )(rows, inverse, mean)


def unpack_kernel(best_ref, slot_ref, out_ref):
    best = best_ref[...]
    owners = best.shape[0]
    count = slot_ref.shape[1]
    slot = slot_ref[...]
    rank = jnp.broadcast_to(slot % CAP, (CAP, count))
    pick = jnp.where(lax.broadcasted_iota(jnp.int32, (CAP, count), 0) == rank, 1.0, 0.0)
    table = nn(best, pick.astype(F32), HIGHEST)
    owner = jnp.broadcast_to(slot // CAP, (owners, count))
    mine = lax.broadcasted_iota(jnp.int32, (owners, count), 0) == owner
    out_ref[...] = jnp.sum(jnp.where(mine, table, 0.0), axis=0, keepdims=True)


def unpack(best, slot):
    return pl.pallas_call(
        unpack_kernel,
        out_shape=jax.ShapeDtypeStruct(slot.shape, F32),
        in_specs=[VM, VM],
        out_specs=VM,
        compiler_params=PARAMS,
        name="unpack",
    )(best, slot)


def exchange(x, axis):
    return lax.all_to_all(x, axis, split_axis=0, concat_axis=0, tiled=True)


def sum_parts(x, count):
    share = x.size // (count * LANES)
    if count % 2 == 0:
        x = jnp.sum(x.reshape(count // 2, 2 * share, LANES), axis=0)
        count = 2
    return jnp.sum(x.reshape(count, share, LANES), axis=0)


def copies_of(x, count):
    return jnp.broadcast_to(x[None, :, None, :], (count, x.shape[0], 1, LANES))


def on_device(embeddings, cluster_id, row_index):
    count = embeddings.shape[0]
    size = {axis: lax.axis_size(axis) for axis in AXES}
    owners = size["y"] * size["core"]
    total_rows = count
    for axis in AXES:
        total_rows = total_rows * size[axis]
    shard, plane = ("y", "core"), ("x_hi", "x_lo", "z_lo", "y")
    swap = [(0, 1), (1, 0)]
    core = lax.axis_index("core").astype(jnp.int32)
    half = lax.axis_index("x_hi").astype(jnp.int32)
    keep, send = moments(core.reshape(1), embeddings)
    pair = keep + lax.ppermute(send, "core", swap)
    near_shares = size["x_lo"] * size["z_lo"] * size["y"]
    shares = size["x_hi"] * near_shares
    pair, embeddings = lax.optimization_barrier((pair, embeddings))
    spread = exchange(pair.reshape(shares, HALF // shares, 1, LANES), plane)
    packed, slot = pack(embeddings, cluster_id, row_index, owners)
    part = sum_parts(spread, shares)
    part, packed = lax.optimization_barrier((part, packed))
    total = sum_parts(exchange(copies_of(part, size["z_hi"]), "z_hi"), size["z_hi"])
    near = exchange(copies_of(total, near_shares), plane[1:]).reshape(PART, LANES)
    rows = exchange(packed.reshape(owners, CAP, WIDE), shard).reshape(owners * CAP, WIDE)
    columns = size["x_hi"] * size["x_lo"]
    far = lax.ppermute(near, plane[:2], [(i, columns - 1 - i) for i in range(columns)])
    near2 = lax.ppermute(near, "core", swap)
    far2 = lax.ppermute(far, "core", swap)
    place = jnp.stack([core, half])
    inverse, mean = factor(place, (near, far, near2, far2), total_rows)
    best = best_of(rows, inverse, mean)
    returned = exchange(best, shard)
    return unpack(returned, slot).reshape(count)


def solution(mesh):
    split = Mesh(mesh.devices.reshape(GROUP_SPLIT + (-1, 2)), AXES)
    return jax.shard_map(
        on_device,
        mesh=split,
        in_specs=(P(AXES, None), P(AXES), P(AXES)),
        out_specs=P(AXES),
        check_vma=False,
    )
```

```python
import functools

import jax
import jax.numpy as jnp
from jax import lax
from jax.experimental import pallas as pl
from jax.experimental.pallas import tpu as pltpu
from jax.sharding import Mesh, PartitionSpec as P

F32 = jnp.float32
BF16 = jnp.bfloat16
FEAT = 768
BLK = 64
NBLK = FEAT // BLK
PANELS = BLK // 8
LANES = 128
WHOLE = [(i, j) for i in range(NBLK) for j in range((i + 1) // 2)]
PAIRED = [(i, i + 2) for i in range(0, NBLK, 4)]
TILES = len(WHOLE) + len(PAIRED) + 1
HALF = TILES // 2 * BLK
PART = HALF // 2
WIDE = FEAT + LANES
CAP = 64
CL_OWN = 8
INDEX_SPAN = 2**19
PIECES = 2
AXES = ("x_hi", "x_lo", "z_hi", "z_lo", "y", "core")
GROUP_SPLIT = (2, 2, 8, 2)
HIGHEST = lax.Precision.HIGHEST
VM = pl.BlockSpec(memory_space=pltpu.VMEM)
SM = pl.BlockSpec(memory_space=pltpu.SMEM)
ANY = pl.BlockSpec(memory_space=pl.ANY)
HBM = pl.BlockSpec(memory_space=pltpu.HBM)
PARAMS = pltpu.CompilerParams(vmem_limit_bytes=24 * 2**20)


def nt(a, b, precision=None):
    return lax.dot_general(
        a, b, (((1,), (1,)), ((), ())), precision=precision, preferred_element_type=F32
    )


def nn(a, b, precision=None):
    return lax.dot_general(
        a, b, (((1,), (0,)), ((), ())), precision=precision, preferred_element_type=F32
    )


def split3(x):
    high = x.astype(BF16)
    rest = x - high.astype(F32)
    mid = rest.astype(BF16)
    low = (rest - mid.astype(F32)).astype(BF16)
    return high, mid, low


def moments_kernel(core_ref, x_ref, keep_ref, send_ref, tri_ref, sems):
    def put(tile, value):
        at = BLK * (tile % (TILES // 2))
        tri_ref[tile // (TILES // 2), at : at + BLK, :] = value

    x = x_ref[...]
    sums = nn(jnp.ones((8, x.shape[0]), BF16), x)
    put(
        TILES - 1,
        jnp.concatenate(
            [sums[:, LANES * j : LANES * (j + 1)] for j in range(FEAT // LANES)]
            + [jnp.zeros((BLK - 8 * (FEAT // LANES), LANES), F32)],
            axis=0,
        ),
    )
    halves = {}
    for b in range(FEAT // 256):
        left = x[:, 256 * b : 256 * (b + 1)].T
        wide = nn(left, x[:, : 256 * (b + 1)])
        for i in range(4 * b, 4 * b + 4):
            strip = wide[BLK * (i - 4 * b) : BLK * (i - 4 * b + 1), :]
            for j in range((i + 1) // 2):
                put(WHOLE.index((i, j)), strip[:, LANES * j : LANES * (j + 1)])
            if i % 2 == 0:
                halves[i] = strip[:, BLK * i : BLK * (i + 1)]
    for n, (i, j) in enumerate(PAIRED):
        put(len(WHOLE) + n, jnp.concatenate([halves[i], halves[j]], axis=1))
    core = core_ref[0]
    mine = pltpu.make_async_copy(tri_ref.at[core], keep_ref, sems.at[0])
    other = pltpu.make_async_copy(tri_ref.at[1 - core], send_ref, sems.at[1])
    other.start()
    mine.start()
    other.wait()
    mine.wait()


def moments(core, x):
    half = jax.ShapeDtypeStruct((HALF, LANES), F32)
    return pl.pallas_call(
        moments_kernel,
        out_shape=(half, half),
        in_specs=[SM, VM],
        out_specs=(ANY, ANY),
        scratch_shapes=[pltpu.VMEM((2, HALF, LANES), F32), pltpu.SemaphoreType.DMA((2,))],
        compiler_params=PARAMS,
        name="moments",
    )(core, x)


def pack_kernel(x_ref, cluster_ref, index_ref, rows_ref, slot_ref):
    count = x_ref.shape[0]
    slots = rows_ref.shape[0]
    owners = slots // CAP
    cluster = cluster_ref[...]
    owner = cluster // CL_OWN
    member = lax.broadcasted_iota(jnp.int32, (owners, count), 0) == jnp.broadcast_to(
        owner, (owners, count)
    )
    earlier = lax.broadcasted_iota(jnp.int32, (count, count), 0) < lax.broadcasted_iota(
        jnp.int32, (count, count), 1
    )
    prefix = nn(jnp.where(member, 1.0, 0.0).astype(BF16), jnp.where(earlier, 1.0, 0.0).astype(BF16))
    rank = jnp.sum(jnp.where(member, prefix, 0.0), axis=0, keepdims=True).astype(jnp.int32)
    slot = owner * CAP + rank
    slot_ref[...] = slot
    place = jnp.where(
        lax.broadcasted_iota(jnp.int32, (slots, count), 0) == jnp.broadcast_to(slot, (slots, count)),
        1.0,
        0.0,
    ).astype(BF16)
    rows_ref[:, :FEAT] = nn(place, x_ref[...]).astype(BF16)
    digit = lax.broadcasted_iota(jnp.int32, (LANES, count), 0)
    whole = jnp.broadcast_to(cluster * INDEX_SPAN + index_ref[...], (LANES, count))
    parts = jnp.where(digit < 4, (whole >> (7 * jnp.minimum(digit, 3))) & 127, 1)
    rows_ref[:, FEAT:] = nt(place, parts.astype(F32).astype(BF16)).astype(BF16)


def pack(x, cluster_id, row_index, owners):
    count = x.shape[0]
    slots = owners * CAP
    return pl.pallas_call(
        pack_kernel,
        out_shape=(
            jax.ShapeDtypeStruct((slots, WIDE), BF16),
            jax.ShapeDtypeStruct((1, count), jnp.int32),
        ),
        in_specs=[VM, VM, VM],
        out_specs=(VM, VM),
        compiler_params=PARAMS,
        name="pack_rows",
    )(x, cluster_id.reshape(1, count), row_index.reshape(1, count))


def inverse_factor(block, spot_ref):
    lane = lax.broadcasted_iota(jnp.int32, (8, LANES), 1)
    sub = lax.broadcasted_iota(jnp.int32, (8, LANES), 0)
    wide = jnp.concatenate([block, jnp.zeros((BLK, BLK), F32)], axis=1)
    a = [
        jnp.where(lane < BLK, wide[8 * g : 8 * g + 8], jnp.where(lane == sub + 8 * g + BLK, 1.0, 0.0))
        for g in range(PANELS)
    ]
    out = []

    def row(x, k):
        return jnp.broadcast_to(x[k : k + 1, :], (8, LANES))

    def column(x, k):
        return jnp.broadcast_to(x[:, k : k + 1], (8, LANES))

    for g in range(PANELS):
        d = [column(a[g], 8 * g + k) for k in range(8)]
        m = {h: [column(a[h], 8 * g + k) for k in range(8)] for h in range(g + 1, PANELS)}
        base = 64 * (g % 2)
        for l in range(8):
            spot_ref[base + 8 * l : base + 8 * l + 8, :] = d[l]
        s = {
            (k, l): jnp.broadcast_to(spot_ref[base + 8 * l + k : base + 8 * l + k + 1, :], (8, LANES))
            for k in range(8)
            for l in range(k, 8)
        }
        scale = [None] * 8
        for k in range(0, 8, 2):
            p, q, t = s[k, k], s[k, k + 1], s[k + 1, k + 1]
            det = p * t - q * q
            over = pl.reciprocal(det, approx=True)
            ua = {l: s[k, l] * t - s[k + 1, l] * q for l in range(k + 2, 8)}
            ub = {l: s[k + 1, l] * p - s[k, l] * q for l in range(k + 2, 8)}
            for l in range(k + 2, 8):
                for n in range(l, 8):
                    num = ua[l] * s[k, n] + ub[l] * s[k + 1, n]
                    s[l, n] = s[l, n] - num * over
            root = lax.rsqrt(p)
            scale[k] = root
            scale[k + 1] = lax.rsqrt(det) * (p * root)
            a0, a1 = row(a[g], k), row(a[g], k + 1)
            va = (a0 * t - a1 * q) * over
            vb = (a1 * p - a0 * q) * over
            sa = {l: ua[l] * over for l in ua}
            sb = {l: ub[l] * over for l in ub}
            ma = jnp.where(sub > k + 1, d[k], 0.0)
            mb = jnp.where(sub > k + 1, d[k + 1], 0.0)
            for l in range(k + 2, 8):
                d[l] = d[l] - (ma * sa[l] + mb * sb[l])
            low = jnp.where(sub == k + 1, q * (root * root), 0.0)
            a[g] = a[g] - (ma * va + mb * vb) - low * a0
            for h in range(g + 1, PANELS):
                ha, hb = m[h][k], m[h][k + 1]
                for l in range(k + 2, 8):
                    m[h][l] = m[h][l] - (ha * sa[l] + hb * sb[l])
                a[h] = a[h] - (ha * va + hb * vb)
        scales = scale[0]
        for k in range(1, 8):
            scales = jnp.where(sub == k, scale[k], scales)
        out.append(a[g] * scales)
    return jnp.concatenate(out, axis=0)[:, BLK:]


def left6(x):
    high, mid, low = split3(x)
    return jnp.concatenate([high, high, mid, mid, high, low], axis=1)


def right6(x, axis):
    high, mid, low = split3(x)
    return jnp.concatenate([high, mid, high, mid, low, high], axis=axis)


def factor_kernel(
    total_rows, place_ref, near_ref, far_ref, near2_ref, far2_ref, out_ref, mean_ref, tri_ref, s_ref, w_ref, leave_ref, spot_ref, sems
):
    core, half = place_ref[0], place_ref[1]
    copies = []
    for side, parts in ((core, (near_ref, far_ref)), (1 - core, (near2_ref, far2_ref))):
        for part, spot in zip(parts, (half, 1 - half)):
            copies.append(
                pltpu.make_async_copy(
                    part, tri_ref.at[side, pl.ds(pl.multiple_of(spot * PART, PART), PART)], sems.at[len(copies)]
                )
            )
    for copy in copies:
        copy.start()
    for copy in copies:
        copy.wait()

    def get(tile):
        at = BLK * (tile % (TILES // 2))
        return tri_ref[tile // (TILES // 2), at : at + BLK, :] * (1.0 / total_rows)

    sums = get(TILES - 1)
    means = [sums[8 * j : 8 * j + 1, :] for j in range(FEAT // LANES)]
    turned = sums.T

    def mean_column(i):
        return turned[BLK * (i % 2) : BLK * (i % 2 + 1), 8 * (i // 2) : 8 * (i // 2) + 1]

    eye = lax.broadcasted_iota(jnp.int32, (BLK, BLK), 0) == lax.broadcasted_iota(
        jnp.int32, (BLK, BLK), 1
    )
    blocks = []
    for i in range(NBLK):
        if i % 2:
            both = get(WHOLE.index((i, i // 2)))[:, BLK:]
            mean = means[i // 2][:, BLK:]
        else:
            n = [pair for pair in PAIRED if i in pair][0]
            both = get(len(WHOLE) + PAIRED.index(n))
            both = both[:, :BLK] if n[0] == i else both[:, BLK:]
            mean = means[i // 2][:, :BLK]
        blocks.append(both - mean_column(i) * mean)
    variance = [jnp.sum(jnp.where(eye, block, 0.0), axis=0, keepdims=True) for block in blocks]
    scale = [
        lax.rsqrt(jnp.concatenate(variance[2 * j : 2 * j + 2], axis=1)) for j in range(FEAT // LANES)
    ]
    upright = jnp.concatenate(
        [jnp.broadcast_to(part, (8, LANES)) for part in scale]
        + [jnp.zeros((BLK - 8 * (FEAT // LANES), LANES), F32)],
        axis=0,
    ).T

    def scale_column(i):
        return upright[BLK * (i % 2) : BLK * (i % 2 + 1), 8 * (i // 2) : 8 * (i // 2) + 1]

    for tile, (i, j) in enumerate(WHOLE):
        s_ref[BLK * i : BLK * (i + 1), LANES * j : LANES * (j + 1)] = (
            (get(tile) - mean_column(i) * means[j]) * scale_column(i) * scale[j]
        )
    for i in range(0, NBLK, 2):
        s_ref[BLK * i : BLK * (i + 1), BLK * i : BLK * (i + 1)] = (
            blocks[i] * scale_column(i) * scale[i // 2][:, :BLK]
        )
    parts = split3(jnp.concatenate(means, axis=1))
    mean_ref[...] = jnp.concatenate(
        [p.astype(F32) for p in parts] + [jnp.zeros((13, FEAT), F32)], axis=0
    ).astype(BF16)

    w_ref[...] = jnp.zeros((FEAT, FEAT), F32)

    def trailing(k, inv6):
        at, to = BLK * k, BLK * (k + 1)
        below = nt(left6(s_ref[to:, at:to]), inv6)
        left, right = left6(below), right6(below, 1)
        for begin in range(0, FEAT - to, 256):
            end = min(begin + 256, FEAT - to)
            skip = BLK if begin == 0 else begin
            if skip < end:
                s_ref[to + skip : to + end, to : to + end] = s_ref[
                    to + skip : to + end, to : to + end
                ] - nt(left[skip:end], right[:end])
        w_ref[to:, :to] = w_ref[to:, :to] - nn(left, right6(w_ref[at:to, :to], 0))

    waiting = None
    leaving = []
    for k in range(NBLK):
        at, to = BLK * k, BLK * (k + 1)
        inv = inverse_factor(s_ref[at:to, at:to], spot_ref)
        if waiting is not None:
            trailing(*waiting)
        inv6 = right6(inv, 1)
        if to < FEAT:
            first = nt(left6(s_ref[to : to + BLK, at:to]), inv6)
            s_ref[to : to + BLK, to : to + BLK] = s_ref[to : to + BLK, to : to + BLK] - nt(
                left6(first), right6(first, 1)
            )
            waiting = (k, inv6)
        if k:
            w_ref[at:to, :at] = nn(left6(inv), right6(w_ref[at:to, :at], 0))
        w_ref[at:to, at:to] = inv
        if to % 256 == 0:
            wide = jnp.concatenate(scale, axis=1)
            leave_ref[to - 256 : to, :to] = w_ref[to - 256 : to, :to] * wide[:, :to]
            copy = pltpu.make_async_copy(
                leave_ref.at[to - 256 : to, 0:to], out_ref.at[to - 256 : to, 0:to], sems.at[to // 256 - 1]
            )
            copy.start()
            leaving.append(copy)
    for copy in leaving:
        copy.wait()


def best_kernel(x_ref, inverse_ref, mean_ref, best_ref, z_ref, u_ref):
    slots = x_ref.shape[0]
    piece = slots // PIECES
    parts = [
        split3(inverse_ref[256 * n : 256 * (n + 1), : 256 * (n + 1)]) for n in range(FEAT // 256)
    ]

    def whiten(x, n):
        high, mid, low = parts[n]
        x = x[:, : 256 * (n + 1)]
        return nt(x, low) + nt(x, mid) + nt(x, high)

    shift = [
        jnp.sum(whiten(mean_ref[...], n), axis=0, keepdims=True) for n in range(FEAT // 256)
    ]
    for i in range(PIECES):
        here = slice(piece * i, piece * (i + 1))
        x = x_ref[here, :FEAT]
        norm = jnp.zeros((piece, 1), F32)
        for n in range(FEAT // 256):
            z = whiten(x, n) - shift[n]
            norm = norm + jnp.sum(z * z, axis=1, keepdims=True)
            z_ref[here, 256 * n : 256 * (n + 1)] = z
        u_ref[here, :] = (z_ref[here, :] * lax.rsqrt(norm + 1e-06)).astype(BF16)

    digits = x_ref[:, FEAT:]
    lane = lax.broadcasted_iota(jnp.int32, (2 * LANES, LANES), 1)
    upper = lax.broadcasted_iota(jnp.int32, (2 * LANES, LANES), 0) >= LANES
    low_weight = jnp.where(lane == 0, 1.0, jnp.where(lane == 1, 128.0, 0.0))
    high_weight = jnp.where(
        lane == 2, 1.0, jnp.where(lane == 3, 128.0, jnp.where(lane == 4, -16384.0, 0.0))
    )
    weight = jnp.where(upper, high_weight, low_weight).astype(BF16)
    down = nt(digits, weight).astype(jnp.int32)
    kkey = down[:, :LANES] + ((down[:, LANES:] + 16384) << 14)
    across = nt(weight, digits).astype(jnp.int32)
    qkey = across[0:1] + ((across[LANES : LANES + 1] + 16384) << 14)
    floor = qkey & ~(INDEX_SPAN - 1)
    best = jnp.full((1, slots), -1.0, F32)
    rows = 256
    for b in range(slots // rows):
        scores = nt(u_ref[rows * b : rows * (b + 1), :], u_ref[...])
        keys = kkey[rows * b : rows * (b + 1), :]
        found = []
        for c in range(0, slots, LANES):
            to = c + LANES
            allowed = (keys < qkey[:, c:to]) & (keys >= floor[:, c:to])
            found.append(
                jnp.max(jnp.where(allowed, scores[:, c:to], -1.0), axis=0, keepdims=True)
            )
        best = jnp.maximum(best, jnp.concatenate(found, axis=1))
    for o in range(slots // CAP):
        best_ref[o : o + 1, :] = best[:, CAP * o : CAP * (o + 1)]


def factor(place, pieces, total_rows):
    return pl.pallas_call(
        functools.partial(factor_kernel, total_rows),
        out_shape=(
            jax.ShapeDtypeStruct((FEAT, FEAT), F32),
            jax.ShapeDtypeStruct((16, FEAT), BF16),
        ),
        in_specs=[SM, ANY, ANY, ANY, ANY],
        out_specs=(HBM, VM),
        scratch_shapes=[
            pltpu.VMEM((2, HALF, LANES), F32),
            pltpu.VMEM((FEAT, FEAT), F32),
            pltpu.VMEM((FEAT, FEAT), F32),
            pltpu.VMEM((FEAT, FEAT), F32),
            pltpu.VMEM((128, LANES), F32),
            pltpu.SemaphoreType.DMA((4,)),
        ],
        compiler_params=PARAMS,
        name="factor",
    )(place, *pieces)


def best_of(rows, inverse, mean):
    slots = rows.shape[0]
    return pl.pallas_call(
        best_kernel,
        out_shape=jax.ShapeDtypeStruct((slots // CAP, CAP), F32),
        in_specs=[VM, VM, VM],
        out_specs=VM,
        scratch_shapes=[pltpu.VMEM((slots, FEAT), F32), pltpu.VMEM((slots, FEAT), BF16)],
        compiler_params=PARAMS,
        name="best",
    )(rows, inverse, mean)


def unpack_kernel(best_ref, slot_ref, out_ref):
    best = best_ref[...]
    owners = best.shape[0]
    count = slot_ref.shape[1]
    slot = slot_ref[...]
    rank = jnp.broadcast_to(slot % CAP, (CAP, count))
    pick = jnp.where(lax.broadcasted_iota(jnp.int32, (CAP, count), 0) == rank, 1.0, 0.0)
    table = nn(best, pick.astype(F32), HIGHEST)
    owner = jnp.broadcast_to(slot // CAP, (owners, count))
    mine = lax.broadcasted_iota(jnp.int32, (owners, count), 0) == owner
    out_ref[...] = jnp.sum(jnp.where(mine, table, 0.0), axis=0, keepdims=True)


def unpack(best, slot):
    return pl.pallas_call(
        unpack_kernel,
        out_shape=jax.ShapeDtypeStruct(slot.shape, F32),
        in_specs=[VM, VM],
        out_specs=VM,
        compiler_params=PARAMS,
        name="unpack",
    )(best, slot)


def exchange(x, axis):
    return lax.all_to_all(x, axis, split_axis=0, concat_axis=0, tiled=True)


def sum_parts(x, count):
    share = x.size // (count * LANES)
    if count % 2 == 0:
        x = jnp.sum(x.reshape(count // 2, 2 * share, LANES), axis=0)
        count = 2
    return jnp.sum(x.reshape(count, share, LANES), axis=0)


def copies_of(x, count):
    return jnp.broadcast_to(x[None, :, None, :], (count, x.shape[0], 1, LANES))


def on_device(embeddings, cluster_id, row_index):
    count = embeddings.shape[0]
    size = {axis: lax.axis_size(axis) for axis in AXES}
    owners = size["y"] * size["core"]
    total_rows = count
    for axis in AXES:
        total_rows = total_rows * size[axis]
    shard, plane = ("y", "core"), ("x_hi", "x_lo", "z_lo", "y")
    swap = [(0, 1), (1, 0)]
    core = lax.axis_index("core").astype(jnp.int32)
    half = lax.axis_index("x_hi").astype(jnp.int32)
    keep, send = moments(core.reshape(1), embeddings)
    pair = keep + lax.ppermute(send, "core", swap)
    near_shares = size["x_lo"] * size["z_lo"] * size["y"]
    shares = size["x_hi"] * near_shares
    pair, embeddings = lax.optimization_barrier((pair, embeddings))
    spread = exchange(pair.reshape(shares, HALF // shares, 1, LANES), plane)
    packed, slot = pack(embeddings, cluster_id, row_index, owners)
    part = sum_parts(spread, shares)
    part, packed = lax.optimization_barrier((part, packed))
    total = sum_parts(exchange(copies_of(part, size["z_hi"]), "z_hi"), size["z_hi"])
    near = exchange(copies_of(total, near_shares), plane[1:]).reshape(PART, LANES)
    rows = exchange(packed.reshape(owners, CAP, WIDE), shard).reshape(owners * CAP, WIDE)
    columns = size["x_hi"] * size["x_lo"]
    far = lax.ppermute(near, plane[:2], [(i, columns - 1 - i) for i in range(columns)])
    near2 = lax.ppermute(near, "core", swap)
    far2 = lax.ppermute(far, "core", swap)
    place = jnp.stack([core, half])
    inverse, mean = factor(place, (near, far, near2, far2), total_rows)
    best = best_of(rows, inverse, mean)
    returned = exchange(best, shard)
    return unpack(returned, slot).reshape(count)


def solution(mesh):
    split = Mesh(mesh.devices.reshape(GROUP_SPLIT + (-1, 2)), AXES)
    return jax.shard_map(
        on_device,
        mesh=split,
        in_specs=(P(AXES, None), P(AXES), P(AXES)),
        out_specs=P(AXES),
        check_vma=False,
    )
```
